256 devices in a mesh: segment: 8 (over z), col: 32 (over y, x, core).
Axes of the slice: x: 4, y: 4, z: 8, core: 2. Of those that a mesh axis runs over, the one named last changes fastest.
Arguments:
- incoming: bfloat16 [8, 4096, 8192], P('segment', 'col'), may hold values from -6 to 6
- hidden: bfloat16 [8, 4096, 14336], P('segment', 'col'), may hold values from -6 to 6
- basis: float32 [8, 8192, 4096], P('segment', None, 'col'), may hold values from -0.0625 to 0.0625
- eigvals: float32 [8, 4096], P('segment', 'col'), may hold values from 0.01 to 1
- query_grads: bfloat16 [8, 128, 8192], P('segment', 'col'), may hold values from -0.0625 to 0.0625
- query_hidden: bfloat16 [8, 128, 14336], P('segment', 'col'), may hold values from -0.046875 to 0.046875
Outputs:
- section_grads: bfloat16 [8, 4096, 8192], P('segment', 'col')
- scores: float32 [64, 8], P('col')
The draws below stay inside these ranges and needn't reach their ends.
All inputs are finite; a program needn't handle non-finite values.
Results may differ from the reference program's by a relative error of at most 0.02.
Values may be sent and summed in bfloat16 or wider, within the bound.
A program may use at most 128 MiB of HBM per device.

```python
import math
import jax
import jax.numpy as jnp
from jax import lax

D = 8192
FFW = 14336
K = 4096
SEQLEN = 64
QUERIES = 8
QLEN = 16
QTOK = 128
TOKENS = 4096
SEQS = 64
LAYERS = 8


def steps_of(own_key, shape, pieces, low, top_value):
    def one(position, parts):
        heights = jax.random.uniform(jax.random.fold_in(jax.random.fold_in(own_key, 6), position), (parts,), jnp.float32, low / len(pieces), top_value / len(pieces))
        return jnp.repeat(jnp.exp(heights), shape[position] // parts).reshape((-1,) + (1,) * (len(shape) - position - 1))

    loudness = one(*pieces[0])
    for cut in pieces[1:]:
        loudness = loudness * one(*cut)
    return loudness


def noise(rng, extent, spread, most, shards=(), kind=jnp.bfloat16):
    values = spread * jax.random.normal(rng, extent, jnp.float32)
    if shards:
        values = values * steps_of(rng, extent, shards, -0.22, 0.18)
    return jnp.clip(values, -most, most).astype(kind)


def setup_inputs(seed: int = 0) -> dict:
    seeds = jax.random.split(jax.random.key(seed), 7)
    return {
        "incoming": noise(seeds[0], (LAYERS, TOKENS, D), 1.0, 6.0, ((0, 8), (1, 32))),
        "hidden": noise(seeds[1], (LAYERS, TOKENS, FFW), 1.0, 6.0, ((0, 8), (1, 32))),
        "basis": noise(seeds[2], (LAYERS, D, K), D ** -0.5, 0.0625, ((0, 8), (2, 32)), jnp.float32),
        "eigvals": jnp.clip(jnp.exp(math.log(1.0) - 4.6051702 * jax.random.uniform(seeds[3], (LAYERS, K), jnp.float32) ** steps_of(seeds[3], (LAYERS, K), ((0, 8), (1, 32)), -0.2, 0.2)), 0.01, 1.0),
        "query_grads": noise(seeds[4], (LAYERS, QTOK, D), D ** -0.5, 0.0625, ((0, 8), (1, 32))),
        "query_hidden": noise(seeds[5], (LAYERS, QTOK, FFW), FFW ** -0.5, 0.046875, ((0, 8), (1, 32))),
    }


damp_ratio = 0.1


def reference(incoming, hidden, basis, eigvals, query_grads, query_hidden):
    section = incoming[LAYERS - 1]
    sections = [None] * LAYERS
    totals = jnp.zeros((SEQS, QUERIES), jnp.float32)
    for layer_index in range(LAYERS - 1, -1, -1):
        if layer_index < LAYERS - 1:
            section = (section.astype(jnp.float32) + incoming[layer_index].astype(jnp.float32)).astype(jnp.bfloat16)
        sections[layer_index] = section
        eigen_vals = eigvals[layer_index]
        damping = damp_ratio * jnp.mean(eigen_vals)
        projected = jnp.dot(basis[layer_index].T, query_grads[layer_index].astype(jnp.float32).T, precision=lax.Precision.HIGHEST)
        weighted = projected / (eigen_vals + damping)[:, None]
        precond = jnp.dot(basis[layer_index], weighted, precision=lax.Precision.HIGHEST).astype(jnp.bfloat16)
        grad_match = jnp.dot(section, precond, preferred_element_type=jnp.float32)
        hidden_match = jnp.dot(hidden[layer_index], query_hidden[layer_index].T, preferred_element_type=jnp.float32)
        products = grad_match * hidden_match
        totals = totals + products.reshape(SEQS, SEQLEN, QUERIES, QLEN).sum(axis=(1, 3)) / (SEQLEN * QLEN)
    return jnp.stack(sections), totals
```

```python
import jax
import jax.numpy as jnp
from jax import lax
from jax.experimental import pallas as pl
from jax.experimental.pallas import tpu as pltpu
from jax.sharding import PartitionSpec as P

D = 8192
F = 14336
K = 4096
SEQLEN = 64
QLEN = 16
DAMP = 0.1

LAYERS = 8
W = 128
NCH = D // W
CHAIN = True
COL = True

f32 = jnp.float32
bf16 = jnp.bfloat16
MESH = pl.DeviceIdType.MESH


def remote(src, dst, ssem, rsem, dev):
    return pltpu.make_async_remote_copy(
        src_ref=src, dst_ref=dst, send_sem=ssem, recv_sem=rsem, device_id=dev, device_id_type=MESH
    )


def split(v):
    hi = v.astype(bf16)
    return hi, (v - hi.astype(f32)).astype(bf16)


def kernel(
    inc, hid, bas, eig, qg, qh,
    out, scores,
    own, rcv, hidv, basv,
    a1g, a1h, qgv, qhv, ebs, ebr,
    part_out, part_in, mine, r1s, r1r, r2s, r2r, prec,
    wmat, accp, gm, hm, share,
    ld_sem, chain_s, chain_r, out_sem, cs, cr, zs, zr,
):
    z = lax.axis_index("segment")
    col = lax.axis_index("col")
    c = lax.rem(col, 2)
    x = lax.rem(col // 2, 4)
    y = col // 8
    a1 = x + c * (y - x)
    a2 = y + c * (x - y)
    step1 = 2 + 6 * c
    step2 = 8 - 6 * c

    def on1(s):
        return (z, col + (lax.rem(a1 + s, 4) - a1) * step1)

    def on2(s):
        return (z, col + (lax.rem(a2 + s, 4) - a2) * step2)

    def onz(s):
        return (lax.rem(z + s, LAYERS), col)

    sibling = (z, col + 1 - 2 * c)
    below = (lax.rem(z + LAYERS - 1, LAYERS), col)

    def load_own(i, _):
        pltpu.make_async_copy(inc.at[0, :, pl.ds(pl.multiple_of(i * W, W), W)], own.at[i], ld_sem.at[0]).start()
        return 0

    lax.fori_loop(0, NCH, load_own, 0)
    load_bas = pltpu.make_async_copy(bas.at[0], basv, ld_sem.at[1])
    load_hid = pltpu.make_async_copy(hid.at[0], hidv, ld_sem.at[2])
    load_bas.start()
    load_hid.start()

    barrier = pltpu.get_barrier_semaphore()
    greeted = [sibling] + [on1(s) for s in (1, 2, 3)] + [on2(s) for s in (1, 2, 3)]
    greeted += [onz(s) for s in range(1, LAYERS)]
    for dev in greeted:
        pl.semaphore_signal(barrier, inc=1, device_id=dev, device_id_type=MESH)
    pl.semaphore_wait(barrier, len(greeted))

    sent = []
    counter = [0]

    def post(src, dst, dev):
        n = counter[0]
        counter[0] += 1
        copy = remote(src, dst, cs.at[n], cr.at[n], dev)
        sent.append(copy)
        copy.start()
        return copy

    def link(i):
        return remote(own.at[i], rcv.at[i], chain_s, chain_r.at[i], below)

    def store_out(i):
        pltpu.make_async_copy(own.at[i], out.at[0, :, pl.ds(pl.multiple_of(i * W, W), W)], out_sem).start()

    def chain_step(t):
        if not CHAIN:
            return
        i = t - 2 * (LAYERS - 1 - z)

        @pl.when(jnp.logical_and(jnp.logical_and(i >= 0, i < NCH), z < LAYERS - 1))
        def _():
            link(i).wait_recv()
            own[i] = (own[i].astype(f32) + rcv[i].astype(f32)).astype(bf16)

            @pl.when(z > 0)
            def _():
                link(i).start()

            store_out(i)

    now = [0]

    def slots(n, fn=None):
        base = now[0]

        def step(j, _):
            chain_step(base + j)
            if fn is not None:
                fn(j)
            return 0

        if not CHAIN and fn is None:
            now[0] += n
            return
        lax.fori_loop(0, n, step, 0)
        now[0] += n

    if COL:
        g1 = [post(qg, a1g.at[pl.ds(a1 * 16, 16)], on1(s)) for s in (1, 2, 3)]
        ebs[0] = jnp.broadcast_to(eig[...], (8, 128))
        e1 = [post(ebs.at[0], ebr.at[s - 1], on1(s)) for s in (1, 2, 3)]
        h1 = [post(qh, a1h.at[pl.ds(a1 * 16, 16)], on1(s)) for s in (1, 2, 3)]

    pltpu.make_async_copy(own, own, ld_sem.at[0]).wait()

    if CHAIN:
        @pl.when(z == LAYERS - 1)
        def _():
            def first(i, _):
                link(i).start()
                return 0

            lax.fori_loop(0, NCH, first, 0)

            def first_out(i, _):
                store_out(i)
                return 0

            lax.fori_loop(0, NCH, first_out, 0)

    def order16():
        r = lax.broadcasted_iota(jnp.int32, (64, 64), 0)
        k = lax.broadcasted_iota(jnp.int32, (64, 64), 1)
        src = ((r % 16) // 4) * 16 + (r % 4) * 4 + r // 16
        return (k == src).astype(f32).astype(bf16)

    def rows16(s):
        return pl.ds(pl.multiple_of(c * 64 + lax.rem(a2 + 4 - s, 4) * 16, 16), 16)

    def assemble(a, q, wide):
        part = jnp.dot(order16(), a[...], preferred_element_type=f32).astype(bf16)
        for s in range(4):
            q[rows16(0), s * wide:(s + 1) * wide] = part[s * 16:(s + 1) * 16]

    def gather2(q):
        second = [post(q.at[rows16(0)], q.at[rows16(0)], on2(s)) for s in (1, 2, 3)]
        swaps = [post(q.at[rows16(0)], q.at[rows16(0)], sibling)]
        return second, swaps

    if COL:
        a1g[pl.ds(pl.multiple_of(a1 * 16, 16), 16)] = qg[...]
        a1h[pl.ds(pl.multiple_of(a1 * 16, 16), 16)] = qh[...]
        slots(2)
        for copy in g1:
            copy.wait_recv()
        assemble(a1g, qgv, D // 4)
        g2, g3 = gather2(qgv)
        for copy in e1:
            copy.wait_recv()
        ebs[1] = ebs[0] + ebr[0] + ebr[1] + ebr[2]
        e2 = [post(ebs.at[1], ebr.at[2 + s], on2(s)) for s in (1, 2, 3)]
        slots(2)
        for copy in h1:
            copy.wait_recv()
        assemble(a1h, qhv, F // 4)
        for copy in e2:
            copy.wait_recv()
        ebs[2] = ebs[1] + ebr[3] + ebr[4] + ebr[5]
        e3 = post(ebs.at[2], ebr.at[6], sibling)
        for s in (1, 3, 2):
            slots(3)
            g2[s - 1].wait_recv()
            g3.append(post(qgv.at[rows16(s)], qgv.at[rows16(s)], sibling))
        h2, h3 = gather2(qhv)
        slots(2)
        load_bas.wait()
        for copy in g3:
            copy.wait_recv()
        e3.wait_recv()
        ebs[3] = ebs[2] + ebr[6]

        KB = 512
        accp[...] = jnp.zeros_like(accp)

        def project(j):
            at = pl.ds(pl.multiple_of(j * KB, KB), KB)
            hi, lo = split(basv[at])
            accp[...] += jnp.dot(qgv[:, at], jnp.concatenate([hi, lo], axis=1), preferred_element_type=f32)

        def project2(j):
            project(2 * j)
            project(2 * j + 1)

        slots(D // KB // 2, project2)
        damping = DAMP * jnp.sum(ebs[3][0:1], axis=1, keepdims=True) / K
        weighted = (accp[:, :128] + accp[:, 128:]) / (eig[...] + damping)
        hi, lo = split(weighted.T)
        wmat[0:128, 0:128] = hi
        wmat[128:256, 0:128] = hi
        wmat[0:128, 128:256] = lo
        wmat[128:256, 128:256] = jnp.zeros_like(lo)

        def expand(row):
            at = pl.ds(pl.multiple_of(row, KB), KB)
            hi, lo = split(basv[at])
            both = jnp.dot(jnp.concatenate([hi, lo], axis=1), wmat[...], preferred_element_type=f32)
            return both[:, :128] + both[:, 128:]

        pair = []
        for b in (1, 3, 2, 0):
            block = lax.rem(a2 + b, 4)

            def give(j, block=block):
                row = block * 1024 + j * KB
                part_out[pl.ds(pl.multiple_of(row, KB), KB)] = expand((1 - c) * 4096 + row).astype(bf16)

            slots(2, give)
            at = pl.ds(pl.multiple_of(block * 1024, 1024), 1024)
            pair.append(post(part_out.at[at], part_in.at[at], sibling))

        def keep(j):
            for half in (0, 1):
                row = (2 * j + half) * KB
                mine[pl.ds(pl.multiple_of(row, KB), KB)] = expand(c * 4096 + row)

        slots(4, keep)

        r1 = []
        for arrival, s in zip(pair, (1, 3, 2, 0)):
            block = lax.rem(a1 + s, 4)
            arrival.wait_recv()

            def add_pair(j, block=block):
                at = pl.ds(pl.multiple_of(block * 1024 + j * KB, KB), KB)
                total = mine[at] + part_in[at].astype(f32)
                mine[at] = total
                r1s[at] = total.astype(bf16)

            slots(2, add_pair)
            if s:
                at = pl.ds(pl.multiple_of(block * 1024, 1024), 1024)
                r1.append(post(r1s.at[at], r1r.at[s - 1], on1(s)))

        for s in (1, 3, 2):
            h2[s - 1].wait_recv()
            h3.append(post(qhv.at[rows16(s)], qhv.at[rows16(s)], sibling))
        slots(3)
        load_hid.wait()
        for copy in h3:
            copy.wait_recv()
        hm[...] = jnp.zeros_like(hm)

        def match_hidden(j):
            for half in range(4):
                at = pl.ds(pl.multiple_of((4 * j + half) * 512, 512), 512)
                hm[...] += lax.dot_general(
                    hidv[:, at], qhv[:, at], (((1,), (1,)), ((), ())), preferred_element_type=f32
                )

        slots(F // 2048, match_hidden)

        for copy in r1:
            copy.wait_recv()
        for s in (1, 3, 2, 0):
            sub = lax.rem(a2 + s, 4)
            at = pl.ds(pl.multiple_of(sub * 256, 256), 256)
            row = pl.ds(pl.multiple_of(a1 * 1024 + sub * 256, 256), 256)
            total = mine[row] + r1r[0, at].astype(f32) + r1r[1, at].astype(f32) + r1r[2, at].astype(f32)
            mine[row] = total
            r2s[at] = total.astype(bf16)
            if s == 1:
                r2 = []
            if s:
                r2.append(post(r2s.at[at], r2r.at[s - 1], on2(s)))
        slots(2)
        for copy in r2:
            copy.wait_recv()
        row = pl.ds(pl.multiple_of(a1 * 1024 + a2 * 256, 256), 256)
        total = mine[row] + r2r[0].astype(f32) + r2r[1].astype(f32) + r2r[2].astype(f32)
        own_rows = pl.ds(pl.multiple_of(c * 4096 + a1 * 1024 + a2 * 256, 256), 256)
        prec[own_rows] = total.astype(bf16)
        p1 = [post(prec.at[own_rows], prec.at[own_rows], on2(s)) for s in (1, 2, 3)]
        slots(2)
        for copy in p1:
            copy.wait_recv()

        def band(s):
            return pl.ds(pl.multiple_of(c * 4096 + lax.rem(a1 + 4 - s, 4) * 1024, 1024), 1024)

        p2 = [post(prec.at[band(0)], prec.at[band(0)], on1(s)) for s in (1, 2, 3)]
        p3 = [post(prec.at[band(0)], prec.at[band(0)], sibling)]
        for s in (1, 3, 2):
            slots(3)
            p2[s - 1].wait_recv()
            p3.append(post(prec.at[band(s)], prec.at[band(s)], sibling))
        slots(1)
        for copy in p3:
            copy.wait_recv()
    else:
        load_bas.wait()
        load_hid.wait()

    gm[...] = jnp.zeros_like(gm)
    total_slots = NCH + 2 * (LAYERS - 1)
    rest = total_slots - now[0]
    rest_needed = NCH // 4
    if rest > rest_needed:
        slots(rest - rest_needed)
        rest = rest_needed

    def match_one(i):
        gm[...] += jnp.dot(own[i], prec[pl.ds(pl.multiple_of(i * W, W), W)], preferred_element_type=f32)

    def match_grads(j):
        for k in range(4):
            match_one(4 * j + k)

    if COL:
        slots(rest_needed, match_grads)
    else:
        slots(rest_needed)

    if COL:
        prod = gm[...] * hm[...]
        pos = lax.broadcasted_iota(jnp.int32, (1, 128), 1)
        side = pos // 64
        p2nd = (pos // 16) % 4
        p1st = (pos // 4) % 4
        query = jnp.where(side == 0, p2nd * 2 + p1st // 2, p1st * 2 + p2nd // 2)
        sums = [jnp.sum(prod[s * SEQLEN:(s + 1) * SEQLEN], axis=0, keepdims=True) for s in (0, 1)]
        lane = lax.broadcasted_iota(jnp.int32, (8, 128), 1)
        line = lax.broadcasted_iota(jnp.int32, (8, 128), 0)
        tile = jnp.zeros((8, 128), f32)
        for s in (0, 1):
            for q in range(8):
                one = jnp.sum(jnp.where(query == q, sums[s], 0.0), axis=1, keepdims=True)
                tile = tile + jnp.where(jnp.logical_and(line == s, lane == q), one, 0.0)
        share[z] = tile / (SEQLEN * QLEN)
        zc = [remote(share.at[z], share.at[z], zs.at[s - 1], zr.at[s - 1], onz(s)) for s in range(1, LAYERS)]
        for copy in zc:
            copy.start()
        for copy in zc:
            copy.wait_recv()
        total = share[0]
        for s in range(1, LAYERS):
            total = total + share[s]
        scores[...] = total[0:2, 0:8]
        for copy in zc:
            copy.wait_send()
    for copy in sent:
        copy.wait_send()
    if CHAIN:
        @pl.when(z > 0)
        def _():
            remote(own, rcv, chain_s, chain_r.at[0], below).wait_send()

        pltpu.make_async_copy(own, own, out_sem).wait()


def column(incoming, hidden, basis, eigvals, query_grads, query_hidden):
    anyspace = pl.BlockSpec(memory_space=pl.ANY)
    vmem = pl.BlockSpec(memory_space=pltpu.VMEM)
    dma = pltpu.SemaphoreType.DMA
    section, scores = pl.pallas_call(
        kernel,
        out_shape=(
            jax.ShapeDtypeStruct((1, 128, D), bf16),
            jax.ShapeDtypeStruct((2, 8), f32),
        ),
        in_specs=[anyspace, anyspace, anyspace, vmem, vmem, vmem],
        out_specs=(anyspace, vmem),
        scratch_shapes=[
            pltpu.VMEM((NCH, 128, W), bf16),
            pltpu.VMEM((NCH, 128, W), bf16),
            pltpu.VMEM((128, F), bf16),
            pltpu.VMEM((D, 128), f32),
            pltpu.VMEM((64, D // 4), bf16),
            pltpu.VMEM((64, F // 4), bf16),
            pltpu.VMEM((128, D), bf16),
            pltpu.VMEM((128, F), bf16),
            pltpu.VMEM((4, 8, 128), f32),
            pltpu.VMEM((7, 8, 128), f32),
            pltpu.VMEM((4096, 128), bf16),
            pltpu.VMEM((4096, 128), bf16),
            pltpu.VMEM((4096, 128), f32),
            pltpu.VMEM((4096, 128), bf16),
            pltpu.VMEM((3, 1024, 128), bf16),
            pltpu.VMEM((1024, 128), bf16),
            pltpu.VMEM((3, 256, 128), bf16),
            pltpu.VMEM((D, 128), bf16),
            pltpu.VMEM((256, 256), bf16),
            pltpu.VMEM((128, 256), f32),
            pltpu.VMEM((128, 128), f32),
            pltpu.VMEM((128, 128), f32),
            pltpu.VMEM((LAYERS, 8, 128), f32),
            dma((3,)),
            dma,
            dma((NCH,)),
            dma,
            dma((48,)),
            dma((48,)),
            dma((LAYERS - 1,)),
            dma((LAYERS - 1,)),
        ],
        compiler_params=pltpu.CompilerParams(
            collective_id=0, has_side_effects=True, vmem_limit_bytes=56 * 1024 * 1024
        ),
    )(
        incoming,
        hidden,
        basis,
        eigvals,
        query_grads.reshape(16, D // 4),
        query_hidden.reshape(16, F // 4),
    )
    return section, scores


def solution(mesh):
    in_specs = (
        P("segment", "col", None),
        P("segment", "col", None),
        P("segment", None, "col"),
        P("segment", "col"),
        P("segment", "col", None),
        P("segment", "col", None),
    )
    out_specs = (P("segment", "col", None), P("col", None))
    return jax.shard_map(column, mesh=mesh, in_specs=in_specs, out_specs=out_specs, check_vma=False)
```

```python
import jax
import jax.numpy as jnp
from jax import lax
from jax.experimental import pallas as pl
from jax.experimental.pallas import tpu as pltpu
from jax.sharding import PartitionSpec as P

D = 8192
F = 14336
K = 4096
SEQLEN = 64
QLEN = 16
DAMP = 0.1

LAYERS = 8
W = 128
NCH = D // W
NZ = 6
NUP = NZ * (LAYERS - 1)
T_G1, T_H1, T_G2, T_G3, T_H2, T_R1, T_R2, T_P1, T_P2 = 6, 9, 15, 20, 32, 42, 47, 53, 61
PER_P = 4
CHAIN = True
COL = True

f32 = jnp.float32
bf16 = jnp.bfloat16
MESH = pl.DeviceIdType.MESH


def remote(src, dst, ssem, rsem, dev):
    return pltpu.make_async_remote_copy(
        src_ref=src, dst_ref=dst, send_sem=ssem, recv_sem=rsem, device_id=dev, device_id_type=MESH
    )


def split(v):
    hi = v.astype(bf16)
    return hi, (v - hi.astype(f32)).astype(bf16)


def kernel(
    inc, hid, bas, eig, qg, qh,
    out, scores,
    own, down, rcv, ups, upr, hidv, basv,
    g16, h16, a1g, a1h, qgv, qhv, ebs, ebr,
    part_out, part_in, mine, r1s, r1r, r2s, r2r, prec,
    wmat, accp, gm, hm, share,
    ld_sem, chain_s, chain_r, up_s, up_r, cs, cr, zs, zr,
):
    z = lax.axis_index("segment")
    col = lax.axis_index("col")
    c = lax.rem(col, 2)
    x = lax.rem(col // 2, 4)
    y = col // 8
    a1 = x + c * (y - x)
    a2 = y + c * (x - y)
    step1 = 2 + 6 * c
    step2 = 8 - 6 * c
    depth = LAYERS - 1 - z

    def on1(s):
        return (z, col + (lax.rem(a1 + s, 4) - a1) * step1)

    def on2(s):
        return (z, col + (lax.rem(a2 + s, 4) - a2) * step2)

    def onz(s):
        return (lax.rem(z + s, LAYERS), col)

    sibling = (z, col + 1 - 2 * c)

    barrier = pltpu.get_barrier_semaphore()
    greeted = [sibling] + [on1(s) for s in (1, 2, 3)] + [on2(s) for s in (1, 2, 3)]
    greeted += [onz(s) for s in range(1, LAYERS)]
    for dev in greeted:
        pl.semaphore_signal(barrier, inc=1, device_id=dev, device_id_type=MESH)

    load_own = pltpu.make_async_copy(inc.at[0], own, ld_sem.at[0])
    load_bas = pltpu.make_async_copy(bas.at[0], basv, ld_sem.at[1])
    load_hid = pltpu.make_async_copy(hid.at[0], hidv, ld_sem.at[2])
    load_own.start()
    load_bas.start()
    load_hid.start()

    def fold(q, wide):
        rows = q[0].astype(f32)
        return jnp.concatenate([rows[:, s * wide:(s + 1) * wide] for s in range(4)], axis=0).astype(bf16)

    g16[...] = fold(qg, D // 4)
    h16[...] = fold(qh, F // 4)
    ebs[0] = jnp.broadcast_to(eig[...], (8, 128))
    pl.semaphore_wait(barrier, len(greeted))

    sent = []
    counter = [0]

    def post(src, dst, dev):
        n = counter[0]
        counter[0] += 1
        copy = remote(src, dst, cs.at[n], cr.at[n], dev)
        sent.append(copy)
        copy.start()
        return copy

    def link(i):
        return remote(down.at[i], rcv.at[i], chain_s, chain_r.at[i], onz(LAYERS - 1))

    def uplink(i):
        return remote(ups.at[i], upr.at[i], up_s, up_r.at[i], onz(1))

    def lanes(i):
        return pl.ds(pl.multiple_of(i * W, W), W)

    def add(p, q):
        return (p.astype(f32) + q.astype(f32)).astype(bf16)

    def chunk_at(t):
        return lax.rem(t + NCH - NZ * depth, NCH)

    def chain_step(t):
        i = chunk_at(t)
        fed = jnp.logical_and(z < LAYERS - 1, t >= NZ)

        @pl.when(fed)
        def _():
            link(i).wait_recv()
            down[i] = add(own[:, lanes(i)], rcv[i])

        @pl.when(jnp.logical_not(fed))
        def _():
            down[i] = own[:, lanes(i)]

        @pl.when(jnp.logical_and(z > 0, t < NCH - NZ))
        def _():
            link(i).start()

        partial = t < NZ * depth

        @pl.when(jnp.logical_not(partial))
        def _():
            out[0, :, lanes(i)] = down[i]

        @pl.when(jnp.logical_and(partial, t // NZ >= 4))
        def _():
            out[0, :, lanes(i)] = add(down[i], upr[i - (NCH - NUP)])

    def up_step(t):
        hop = t // NZ
        cut = lax.rem(z - hop + LAYERS, LAYERS)

        @pl.when(cut > 0)
        def _():
            n = (cut - 1) * NZ + t - hop * NZ
            i = NCH - NUP + n
            last = hop == LAYERS - 1

            @pl.when(hop > 0)
            def _():
                uplink(n).wait_recv()

            @pl.when(jnp.logical_and(z >= cut, hop > 0))
            def _():
                ups[n] = add(own[:, lanes(i)], upr[n])

            @pl.when(jnp.logical_and(z >= cut, hop == 0))
            def _():
                ups[n] = own[:, lanes(i)]

            @pl.when(jnp.logical_and(z < cut, jnp.logical_not(last)))
            def _():
                ups[n] = upr[n]

            @pl.when(jnp.logical_not(last))
            def _():
                uplink(n).start()

            @pl.when(jnp.logical_and(z < cut, cut - z <= 4))
            def _():
                out[0, :, lanes(i)] = add(down[i], upr[n])

    now = [0]

    def slots(n, fn=None):
        if not CHAIN:
            now[0] = max(now[0], min(now[0] + n, NCH))
            if fn is not None:
                def plain(j, _):
                    fn(j)
                    return 0

                lax.fori_loop(0, n, plain, 0)
            return
        done = 0
        while done < n:
            base = now[0]
            stop = n - done
            if base < NZ * LAYERS:
                stop = min(stop, NZ * LAYERS - base)
            elif base < NCH:
                stop = min(stop, NCH - base)
            elif fn is None:
                return

            def step(j, _, base=base, done=done):
                if base < NCH:
                    chain_step(base + j)
                if base < NZ * LAYERS:
                    up_step(base + j)
                if fn is not None:
                    fn(done + j)
                return 0

            lax.fori_loop(0, stop, step, 0)
            now[0] += stop
            done += stop

    def until(t):
        if now[0] < t:
            slots(t - now[0])

    if COL:
        g1 = [post(g16, a1g.at[pl.ds(a1 * 16, 16)], on1(s)) for s in (1, 2, 3)]
        e1 = [post(ebs.at[0], ebr.at[s - 1], on1(s)) for s in (1, 2, 3)]
        h1 = [post(h16, a1h.at[pl.ds(a1 * 16, 16)], on1(s)) for s in (1, 2, 3)]

    load_own.wait()

    def order16():
        r = lax.broadcasted_iota(jnp.int32, (64, 64), 0)
        k = lax.broadcasted_iota(jnp.int32, (64, 64), 1)
        src = ((r % 16) // 4) * 16 + (r // 16) * 4 + r % 4
        return (k == src).astype(f32).astype(bf16)

    def rows16(s):
        return pl.ds(pl.multiple_of(c * 64 + lax.rem(a2 + 4 - s, 4) * 16, 16), 16)

    def assemble(a, q, wide):
        part = jnp.dot(order16(), a[...], preferred_element_type=f32).astype(bf16)
        for s in range(4):
            q[rows16(0), s * wide:(s + 1) * wide] = part[s * 16:(s + 1) * 16]

    def gather2(q):
        second = [post(q.at[rows16(0)], q.at[rows16(0)], on2(s)) for s in (1, 2, 3)]
        swaps = [post(q.at[rows16(0)], q.at[rows16(0)], sibling)]
        return second, swaps

    if COL:
        a1g[pl.ds(pl.multiple_of(a1 * 16, 16), 16)] = g16[...]
        a1h[pl.ds(pl.multiple_of(a1 * 16, 16), 16)] = h16[...]
        until(T_G1)
        for copy in g1:
            copy.wait_recv()
        assemble(a1g, qgv, D // 4)
        g2, g3 = gather2(qgv)
        for copy in e1:
            copy.wait_recv()
        ebs[1] = ebs[0] + ebr[0] + ebr[1] + ebr[2]
        e2 = [post(ebs.at[1], ebr.at[2 + s], on2(s)) for s in (1, 2, 3)]
        until(T_H1)
        for copy in h1:
            copy.wait_recv()
        assemble(a1h, qhv, F // 4)
        for copy in e2:
            copy.wait_recv()
        ebs[2] = ebs[1] + ebr[3] + ebr[4] + ebr[5]
        e3 = post(ebs.at[2], ebr.at[6], sibling)
        until(T_G2)
        h2, h3 = gather2(qhv)
        for s, t in zip((1, 3, 2), (T_G2, T_G2 + 1, T_G2 + 2)):
            until(t)
            g2[s - 1].wait_recv()
            g3.append(post(qgv.at[rows16(s)], qgv.at[rows16(s)], sibling))
        until(T_G3)
        load_bas.wait()
        for copy in g3:
            copy.wait_recv()
        e3.wait_recv()
        ebs[3] = ebs[2] + ebr[6]

        KB = 512
        accp[...] = jnp.zeros_like(accp)

        def project(j):
            for k in range(PER_P):
                at = pl.ds(pl.multiple_of((PER_P * j + k) * KB, KB), KB)
                hi, lo = split(basv[at])
                accp[...] += jnp.dot(qgv[:, at], jnp.concatenate([hi, lo], axis=1), preferred_element_type=f32)

        slots(D // KB // PER_P, project)
        damping = DAMP * jnp.sum(ebs[3][0:1], axis=1, keepdims=True) / K
        weighted = (accp[:, :128] + accp[:, 128:]) / (eig[...] + damping)
        hi, lo = split(weighted.T)
        wmat[0:128, 0:128] = hi
        wmat[128:256, 0:128] = hi
        wmat[0:128, 128:256] = lo
        wmat[128:256, 128:256] = jnp.zeros_like(lo)

        def expand(row):
            at = pl.ds(pl.multiple_of(row, KB), KB)
            hi, lo = split(basv[at])
            both = jnp.dot(jnp.concatenate([hi, lo], axis=1), wmat[...], preferred_element_type=f32)
            return both[:, :128] + both[:, 128:]

        pair = []
        for b in (1, 3, 2, 0):
            block = lax.rem(a2 + b, 4)

            def give(j, block=block):
                for k in range(2):
                    row = block * 1024 + (2 * j + k) * KB
                    part_out[pl.ds(pl.multiple_of(row, KB), KB)] = expand((1 - c) * 4096 + row).astype(bf16)

            slots(1, give)
            at = pl.ds(pl.multiple_of(block * 1024, 1024), 1024)
            pair.append(post(part_out.at[at], part_in.at[at], sibling))

        r1 = []
        for arrival, s in zip(pair, (1, 3, 2, 0)):
            block = lax.rem(a1 + s, 4)

            def keep(j, block=block):
                for k in range(2):
                    row = block * 1024 + (2 * j + k) * KB
                    mine[pl.ds(pl.multiple_of(row, KB), KB)] = expand(c * 4096 + row)

            slots(1, keep)
            arrival.wait_recv()
            at = pl.ds(pl.multiple_of(block * 1024, 1024), 1024)
            total = mine[at] + part_in[at].astype(f32)
            if s:
                r1s[at] = total.astype(bf16)
                r1.append(post(r1s.at[at], r1r.at[s - 1], on1(s)))
            else:
                mine[at] = total

        until(T_H2)
        for s in (1, 3, 2):
            h2[s - 1].wait_recv()
            h3.append(post(qhv.at[rows16(s)], qhv.at[rows16(s)], sibling))
            slots(1)
        load_hid.wait()
        for copy in h3:
            copy.wait_recv()
        hm[...] = jnp.zeros_like(hm)

        def match_hidden(j):
            for half in range(4):
                at = pl.ds(pl.multiple_of((4 * j + half) * 512, 512), 512)
                hm[...] += lax.dot_general(
                    hidv[:, at], qhv[:, at], (((1,), (1,)), ((), ())), preferred_element_type=f32
                )

        slots(F // 2048, match_hidden)

        until(T_R1)
        for copy in r1:
            copy.wait_recv()
        r2 = []
        for s in (1, 3, 2, 0):
            sub = lax.rem(a2 + s, 4)
            at = pl.ds(pl.multiple_of(sub * 256, 256), 256)
            row = pl.ds(pl.multiple_of(a1 * 1024 + sub * 256, 256), 256)
            total = mine[row] + r1r[0, at].astype(f32) + r1r[1, at].astype(f32) + r1r[2, at].astype(f32)
            if s:
                r2s[at] = total.astype(bf16)
                r2.append(post(r2s.at[at], r2r.at[s - 1], on2(s)))
            else:
                mine[row] = total
        until(T_R2)
        for copy in r2:
            copy.wait_recv()
        row = pl.ds(pl.multiple_of(a1 * 1024 + a2 * 256, 256), 256)
        total = mine[row] + r2r[0].astype(f32) + r2r[1].astype(f32) + r2r[2].astype(f32)
        own_rows = pl.ds(pl.multiple_of(c * 4096 + a1 * 1024 + a2 * 256, 256), 256)
        prec[own_rows] = total.astype(bf16)
        p1 = [post(prec.at[own_rows], prec.at[own_rows], on2(s)) for s in (1, 2, 3)]
        until(T_P1)
        for copy in p1:
            copy.wait_recv()

        def band(s):
            return pl.ds(pl.multiple_of(c * 4096 + lax.rem(a1 + 4 - s, 4) * 1024, 1024), 1024)

        p2 = [post(prec.at[band(0)], prec.at[band(0)], on1(s)) for s in (1, 2, 3)]
        p3 = {0: post(prec.at[band(0)], prec.at[band(0)], sibling)}

        gm[...] = jnp.zeros_like(gm)

        def match_one(i):
            gm[...] += jnp.dot(
                out[0, :, lanes(i)], prec[pl.ds(pl.multiple_of(i * W, W), W)], preferred_element_type=f32
            )

        def first_chunk(mine_half, s):
            side, at = (c, a1) if mine_half else (1 - c, a2)
            return side * (NCH // 2) + lax.rem(at + 4 - s, 4) * 8

        def match_band(mine_half, s, wait=0):
            first = first_chunk(mine_half, s)
            seen = now[0]

            def pair_of(j):
                for k in (0, 1):
                    i = first + 2 * j + k
                    if seen >= NCH or not CHAIN:
                        match_one(i)
                    else:
                        @pl.when(lax.rem(i + NZ * depth, NCH) < seen)
                        def _(i=i):
                            match_one(i)

            slots(4, pair_of)
            return seen

        began = {}
        began[True, 0] = match_band(True, 0)
        p3[0].wait_recv()
        began[False, 0] = match_band(False, 0)
        until(T_P2)
        for s in (1, 3):
            p2[s - 1].wait_recv()
            p3[s] = post(prec.at[band(s)], prec.at[band(s)], sibling)
        began[True, 1] = match_band(True, 1)
        began[True, 3] = match_band(True, 3)
        p3[1].wait_recv()
        began[False, 1] = match_band(False, 1)
        p2[1].wait_recv()
        p3[2] = post(prec.at[band(2)], prec.at[band(2)], sibling)
        p3[3].wait_recv()
        began[False, 3] = match_band(False, 3)
        until(NCH)
        began[True, 2] = match_band(True, 2)
        p3[2].wait_recv()
        began[False, 2] = match_band(False, 2)

        if CHAIN:
            for (mine_half, s), seen in began.items():
                if seen < NCH:
                    first = first_chunk(mine_half, s)

                    def late(j, _, first=first, seen=seen):
                        i = first + j

                        @pl.when(lax.rem(i + NZ * depth, NCH) >= seen)
                        def _():
                            match_one(i)

                        return 0

                    lax.fori_loop(0, 8, late, 0)
    else:
        load_bas.wait()
        load_hid.wait()
        until(NCH)

    if COL:
        prod = gm[...] * hm[...]
        pos = lax.broadcasted_iota(jnp.int32, (1, 128), 1)
        side = pos // 64
        p2nd = (pos // 16) % 4
        p1st = (pos // 4) % 4
        query = jnp.where(side == 0, p2nd * 2 + p1st // 2, p1st * 2 + p2nd // 2)
        sums = [jnp.sum(prod[s * SEQLEN:(s + 1) * SEQLEN], axis=0, keepdims=True) for s in (0, 1)]
        lane = lax.broadcasted_iota(jnp.int32, (8, 128), 1)
        line = lax.broadcasted_iota(jnp.int32, (8, 128), 0)
        tile = jnp.zeros((8, 128), f32)
        for s in (0, 1):
            for q in range(8):
                one = jnp.sum(jnp.where(query == q, sums[s], 0.0), axis=1, keepdims=True)
                tile = tile + jnp.where(jnp.logical_and(line == s, lane == q), one, 0.0)
        share[z] = tile / (SEQLEN * QLEN)
        zc = [remote(share.at[z], share.at[z], zs.at[s - 1], zr.at[s - 1], onz(s)) for s in range(1, LAYERS)]
        for copy in zc:
            copy.start()
        for copy in sent:
            copy.wait_send()
    if CHAIN:
        @pl.when(z > 0)
        def _():
            sends = pl.ds(0, NCH - NZ)
            remote(down.at[sends], rcv.at[sends], chain_s, chain_r.at[0], onz(LAYERS - 1)).wait_send()

        @pl.when(z < LAYERS - 1)
        def _():
            sends = pl.ds(0, NUP - NZ)
            remote(ups.at[sends], upr.at[sends], up_s, up_r.at[0], onz(1)).wait_send()

        @pl.when(z == LAYERS - 1)
        def _():
            remote(ups, upr, up_s, up_r.at[0], onz(1)).wait_send()

    if COL:
        for copy in zc:
            copy.wait_recv()
        total = share[0]
        for s in range(1, LAYERS):
            total = total + share[s]
        scores[...] = total[0:2, 0:8]
        for copy in zc:
            copy.wait_send()


def column(incoming, hidden, basis, eigvals, query_grads, query_hidden):
    hbm = pl.BlockSpec(memory_space=pltpu.HBM)
    vmem = pl.BlockSpec(memory_space=pltpu.VMEM)
    dma = pltpu.SemaphoreType.DMA
    section, scores = pl.pallas_call(
        kernel,
        out_shape=(
            pltpu.VMEM((1, 128, D), bf16),
            pltpu.VMEM((2, 8), f32),
        ),
        in_specs=[hbm, hbm, hbm, vmem, vmem, vmem],
        out_specs=(vmem, vmem),
        scratch_shapes=[
            pltpu.VMEM((128, D), bf16),
            pltpu.VMEM((NCH, 128, W), bf16),
            pltpu.VMEM((NCH, 128, W), bf16),
            pltpu.VMEM((NUP, 128, W), bf16),
            pltpu.VMEM((NUP, 128, W), bf16),
            pltpu.VMEM((128, F), bf16),
            pltpu.VMEM((D, 128), f32),
            pltpu.VMEM((16, D // 4), bf16),
            pltpu.VMEM((16, F // 4), bf16),
            pltpu.VMEM((64, D // 4), bf16),
            pltpu.VMEM((64, F // 4), bf16),
            pltpu.VMEM((128, D), bf16),
            pltpu.VMEM((128, F), bf16),
            pltpu.VMEM((4, 8, 128), f32),
            pltpu.VMEM((7, 8, 128), f32),
            pltpu.VMEM((4096, 128), bf16),
            pltpu.VMEM((4096, 128), bf16),
            pltpu.VMEM((4096, 128), f32),
            pltpu.VMEM((4096, 128), bf16),
            pltpu.VMEM((3, 1024, 128), bf16),
            pltpu.VMEM((1024, 128), bf16),
            pltpu.VMEM((3, 256, 128), bf16),
            pltpu.VMEM((D, 128), bf16),
            pltpu.VMEM((256, 256), bf16),
            pltpu.VMEM((128, 256), f32),
            pltpu.VMEM((128, 128), f32),
            pltpu.VMEM((128, 128), f32),
            pltpu.VMEM((LAYERS, 8, 128), f32),
            dma((3,)),
            dma,
            dma((NCH,)),
            dma,
            dma((NUP,)),
            dma((48,)),
            dma((48,)),
            dma((LAYERS - 1,)),
            dma((LAYERS - 1,)),
        ],
        compiler_params=pltpu.CompilerParams(
            collective_id=0, has_side_effects=True, vmem_limit_bytes=60 * 1024 * 1024
        ),
    )(incoming, hidden, basis, eigvals, query_grads, query_hidden)
    return section, scores


def solution(mesh):
    in_specs = (
        P("segment", "col", None),
        P("segment", "col", None),
        P("segment", None, "col"),
        P("segment", "col"),
        P("segment", "col", None),
        P("segment", "col", None),
    )
    out_specs = (P("segment", "col", None), P("col", None))
    return jax.shard_map(column, mesh=mesh, in_specs=in_specs, out_specs=out_specs, check_vma=False)
```

```python
import jax
import jax.numpy as jnp
from jax import lax
from jax.experimental import pallas as pl
from jax.experimental.pallas import tpu as pltpu
from jax.sharding import PartitionSpec as P

D = 8192
F = 14336
K = 4096
SEQLEN = 64
QLEN = 16
DAMP = 0.1

LAYERS = 8
W = 128
NCH = D // W
NZ = 8
NUP = NZ * (LAYERS - 1)
T_G1, T_H1, T_H2S, T_G2, T_G3, T_H2, T_H3 = 8, 10, 15, 22, 24, 35, 37
T_R1 = (38, 42)
T_R2 = (43, 47)
T_P1 = (48, 52)
T_P2 = (56, 60)
PER_P = 8
CHAIN = True
COL = True

f32 = jnp.float32
bf16 = jnp.bfloat16
MESH = pl.DeviceIdType.MESH


def remote(src, dst, ssem, rsem, dev):
    return pltpu.make_async_remote_copy(
        src_ref=src, dst_ref=dst, send_sem=ssem, recv_sem=rsem, device_id=dev, device_id_type=MESH
    )


def split(v):
    hi = v.astype(bf16)
    return hi, (v - hi.astype(f32)).astype(bf16)


def kernel(
    inc, hid, bas, eig, qg, qh,
    out, scores,
    own, down, rcv, ups, upr, hidv, basv,
    g16, h16, a1g, a1h, qgv, qhv, ebs, ebr,
    part_out, part_in, mine, r1s, r1r, r2s, r2r, prec,
    wmat, accp, gm, hm, share,
    ld_sem, chain_s, chain_r, up_s, up_r, cs, cr, zs, zr,
):
    z = lax.axis_index("segment")
    col = lax.axis_index("col")
    c = lax.rem(col, 2)
    x = lax.rem(col // 2, 4)
    y = col // 8
    a1 = x + c * (y - x)
    a2 = y + c * (x - y)
    step1 = 2 + 6 * c
    step2 = 8 - 6 * c
    depth = LAYERS - 1 - z

    def on1(s):
        return (z, col + (lax.rem(a1 + s, 4) - a1) * step1)

    def on2(s):
        return (z, col + (lax.rem(a2 + s, 4) - a2) * step2)

    def onz(s):
        return (lax.rem(z + s, LAYERS), col)

    sibling = (z, col + 1 - 2 * c)

    barrier = pltpu.get_barrier_semaphore()
    greeted = [sibling] + [on1(s) for s in (1, 2, 3)] + [on2(s) for s in (1, 2, 3)]
    greeted += [onz(s) for s in range(1, LAYERS)]
    for dev in greeted:
        pl.semaphore_signal(barrier, inc=1, device_id=dev, device_id_type=MESH)

    load_own = pltpu.make_async_copy(inc.at[0], own, ld_sem.at[0])
    load_bas = pltpu.make_async_copy(bas.at[0], basv, ld_sem.at[1])
    load_hid = pltpu.make_async_copy(hid.at[0], hidv, ld_sem.at[2])
    load_own.start()
    load_bas.start()
    load_hid.start()

    def fold(q, wide):
        rows = q[0].astype(f32)
        return jnp.concatenate([rows[:, s * wide:(s + 1) * wide] for s in range(4)], axis=0).astype(bf16)

    g16[...] = fold(qg, D // 4)
    h16[...] = fold(qh, F // 4)
    ebs[0] = jnp.broadcast_to(eig[...], (8, 128))
    pl.semaphore_wait(barrier, len(greeted))

    sent = []
    counter = [0]

    def post(src, dst, dev):
        n = counter[0]
        counter[0] += 1
        copy = remote(src, dst, cs.at[n], cr.at[n], dev)
        sent.append(copy)
        copy.start()
        return copy

    def link(i):
        return remote(down.at[i], rcv.at[i], chain_s, chain_r.at[i], onz(LAYERS - 1))

    def uplink(i):
        return remote(ups.at[i], upr.at[i], up_s, up_r.at[i], onz(1))

    def lanes(i):
        return pl.ds(pl.multiple_of(i * W, W), W)

    def add(p, q):
        return (p.astype(f32) + q.astype(f32)).astype(bf16)

    def chunk_at(t):
        return lax.rem(t + NCH - NZ * depth, NCH)

    def chain_step(t):
        i = chunk_at(t)
        fed = jnp.logical_and(z < LAYERS - 1, t >= NZ)

        @pl.when(fed)
        def _():
            link(i).wait_recv()
            down[i] = add(own[:, lanes(i)], rcv[i])

        @pl.when(jnp.logical_not(fed))
        def _():
            down[i] = own[:, lanes(i)]

        @pl.when(jnp.logical_and(z > 0, t < NCH - NZ))
        def _():
            link(i).start()

        partial = t < NZ * depth

        @pl.when(jnp.logical_not(partial))
        def _():
            out[0, :, lanes(i)] = down[i]

        @pl.when(jnp.logical_and(partial, t // NZ >= LAYERS // 2))
        def _():
            out[0, :, lanes(i)] = add(down[i], upr[i - (NCH - NUP)])

    def up_step(t):
        hop = t // NZ
        cut = lax.rem(z - hop + LAYERS, LAYERS)

        @pl.when(cut > 0)
        def _():
            n = (cut - 1) * NZ + t - hop * NZ
            i = NCH - NUP + n
            last = hop == LAYERS - 1

            @pl.when(hop > 0)
            def _():
                uplink(n).wait_recv()

            @pl.when(jnp.logical_and(z >= cut, hop > 0))
            def _():
                ups[n] = add(own[:, lanes(i)], upr[n])

            @pl.when(jnp.logical_and(z >= cut, hop == 0))
            def _():
                ups[n] = own[:, lanes(i)]

            @pl.when(jnp.logical_and(z < cut, jnp.logical_not(last)))
            def _():
                ups[n] = upr[n]

            @pl.when(jnp.logical_not(last))
            def _():
                uplink(n).start()

            @pl.when(jnp.logical_and(z < cut, cut - z <= 4))
            def _():
                out[0, :, lanes(i)] = add(down[i], upr[n])

    now = [0]

    def slots(n, fn=None):
        if not CHAIN:
            now[0] = max(now[0], min(now[0] + n, NCH))
            if fn is not None:
                def plain(j, _):
                    fn(j)
                    return 0

                lax.fori_loop(0, n, plain, 0)
            return
        done = 0
        while done < n:
            base = now[0]
            stop = n - done
            if base < NZ * LAYERS:
                stop = min(stop, NZ * LAYERS - base)
            elif base < NCH:
                stop = min(stop, NCH - base)
            elif fn is None:
                return

            def step(j, _, base=base, done=done):
                if base < NCH:
                    chain_step(base + j)
                if base < NZ * LAYERS:
                    up_step(base + j)
                if fn is not None:
                    fn(done + j)
                return 0

            lax.fori_loop(0, stop, step, 0)
            now[0] += stop
            done += stop

    def until(t):
        if now[0] < t:
            slots(t - now[0])

    if COL:
        g1 = [post(g16, a1g.at[pl.ds(a1 * 16, 16)], on1(s)) for s in (1, 2, 3)]
        e1 = [post(ebs.at[0], ebr.at[s - 1], on1(s)) for s in (1, 2, 3)]
        h1 = [post(h16, a1h.at[pl.ds(a1 * 16, 16)], on1(s)) for s in (1, 2, 3)]

    load_own.wait()

    def order16():
        r = lax.broadcasted_iota(jnp.int32, (64, 64), 0)
        k = lax.broadcasted_iota(jnp.int32, (64, 64), 1)
        src = ((r % 16) // 4) * 16 + (r // 16) * 4 + r % 4
        return (k == src).astype(f32).astype(bf16)

    def rows16(s):
        return pl.ds(pl.multiple_of(c * 64 + lax.rem(a2 + 4 - s, 4) * 16, 16), 16)

    def assemble(a, q, wide):
        part = jnp.dot(order16(), a[...], preferred_element_type=f32).astype(bf16)
        for s in range(4):
            q[rows16(0), s * wide:(s + 1) * wide] = part[s * 16:(s + 1) * 16]

    def gather2(q):
        second = [post(q.at[rows16(0)], q.at[rows16(0)], on2(s)) for s in (1, 2, 3)]
        swaps = [post(q.at[rows16(0)], q.at[rows16(0)], sibling)]
        return second, swaps

    if COL:
        a1g[pl.ds(pl.multiple_of(a1 * 16, 16), 16)] = g16[...]
        a1h[pl.ds(pl.multiple_of(a1 * 16, 16), 16)] = h16[...]
        until(T_G1)
        for copy in g1:
            copy.wait_recv()
        assemble(a1g, qgv, D // 4)
        g2, g3 = gather2(qgv)
        for copy in e1:
            copy.wait_recv()
        ebs[1] = ebs[0] + ebr[0] + ebr[1] + ebr[2]
        e2 = [post(ebs.at[1], ebr.at[2 + s], on2(s)) for s in (1, 2, 3)]
        until(T_H1)
        for copy in h1:
            copy.wait_recv()
        assemble(a1h, qhv, F // 4)
        for copy in e2:
            copy.wait_recv()
        ebs[2] = ebs[1] + ebr[3] + ebr[4] + ebr[5]
        e3 = post(ebs.at[2], ebr.at[6], sibling)
        until(T_H2S)
        h2, h3 = gather2(qhv)
        until(T_G2)
        for s in (1, 3, 2):
            g2[s - 1].wait_recv()
            g3.append(post(qgv.at[rows16(s)], qgv.at[rows16(s)], sibling))
        until(T_G3)
        load_bas.wait()
        for copy in g3:
            copy.wait_recv()
        e3.wait_recv()
        ebs[3] = ebs[2] + ebr[6]

        KB = 512
        accp[...] = jnp.zeros_like(accp)

        def project(j):
            for k in range(PER_P):
                at = pl.ds(pl.multiple_of((PER_P * j + k) * KB, KB), KB)
                hi, lo = split(basv[at])
                accp[...] += jnp.dot(qgv[:, at], jnp.concatenate([hi, lo], axis=1), preferred_element_type=f32)

        slots(D // KB // PER_P, project)
        damping = DAMP * jnp.sum(ebs[3][0:1], axis=1, keepdims=True) / K
        weighted = (accp[:, :128] + accp[:, 128:]) / (eig[...] + damping)
        hi, lo = split(weighted.T)
        wmat[0:128, 0:128] = hi
        wmat[128:256, 0:128] = hi
        wmat[0:128, 128:256] = lo
        wmat[128:256, 128:256] = jnp.zeros_like(lo)

        def expand(row):
            at = pl.ds(pl.multiple_of(row, KB), KB)
            hi, lo = split(basv[at])
            both = jnp.dot(jnp.concatenate([hi, lo], axis=1), wmat[...], preferred_element_type=f32)
            return both[:, :128] + both[:, 128:]

        def block_rows(block, half):
            return pl.ds(pl.multiple_of(block * 1024 + half * KB, KB), KB)

        pair = {}
        for half in (0, 1):
            slots(1)
            for s in (1, 3, 2, 0):
                block = lax.rem(a2 + s, 4)
                at = block_rows(block, half)
                part_out[at] = expand((1 - c) * 4096 + block * 1024 + half * KB).astype(bf16)
                pair[half, s] = post(part_out.at[at], part_in.at[at], sibling)

        r1 = {}
        for half in (0, 1):
            slots(1)
            for s in (1, 3, 2, 0):
                block = lax.rem(a1 + s, 4)
                at = block_rows(block, half)
                own_part = expand(c * 4096 + block * 1024 + half * KB)
                pair[half, s].wait_recv()
                total = own_part + part_in[at].astype(f32)
                if s:
                    r1s[at] = total.astype(bf16)
                    r1[half, s] = post(r1s.at[at], r1r.at[s - 1, pl.ds(half * KB, KB)], on1(s))
                else:
                    mine[pl.ds(half * KB, KB)] = total

        def match_hidden(j):
            for k in range(4):
                at = pl.ds(pl.multiple_of((4 * j + k) * 512, 512), 512)
                hm[...] += lax.dot_general(
                    hidv[:, at], qhv[:, at], (((1,), (1,)), ((), ())), preferred_element_type=f32
                )

        r2, p1, p2, p3 = {}, {}, {}, {}

        def sum_first(half):
            for s in (1, 2, 3):
                r1[half, s].wait_recv()
            for s in (1, 3, 2, 0):
                at = pl.ds(pl.multiple_of(half * KB + lax.rem(a2 + s, 4) * 128, 128), 128)
                total = mine[at] + r1r[0, at].astype(f32) + r1r[1, at].astype(f32) + r1r[2, at].astype(f32)
                if s:
                    r2s[at] = total.astype(bf16)
                    r2[half, s] = post(r2s.at[at], r2r.at[s - 1, pl.ds(half * 128, 128)], on2(s))
                else:
                    mine[at] = total

        def sum_second(half):
            for s in (1, 2, 3):
                r2[half, s].wait_recv()
            at = pl.ds(pl.multiple_of(half * KB + a2 * 128, 128), 128)
            got = pl.ds(half * 128, 128)
            total = mine[at] + r2r[0, got].astype(f32) + r2r[1, got].astype(f32) + r2r[2, got].astype(f32)
            rows = pl.ds(pl.multiple_of(c * 4096 + a1 * 1024 + half * KB + a2 * 128, 128), 128)
            prec[rows] = total.astype(bf16)
            for s in (1, 3, 2):
                p1[half, s] = post(prec.at[rows], prec.at[rows], on2(s))

        def band(s, half):
            return pl.ds(pl.multiple_of(c * 4096 + lax.rem(a1 + 4 - s, 4) * 1024 + half * KB, KB), KB)

        def gather_first(half):
            for s in (1, 2, 3):
                p1[half, s].wait_recv()
            rows = band(0, half)
            for s in (1, 3, 2):
                p2[half, s] = post(prec.at[rows], prec.at[rows], on1(s))
            p3[half, 0] = post(prec.at[rows], prec.at[rows], sibling)

        def gather_second(half):
            for s in (1, 3, 2):
                rows = band(s, half)
                p2[half, s].wait_recv()
                p3[half, s] = post(prec.at[rows], prec.at[rows], sibling)

        until(T_H2)
        for s in (1, 3, 2):
            h2[s - 1].wait_recv()
            h3.append(post(qhv.at[rows16(s)], qhv.at[rows16(s)], sibling))
        until(T_R1[0])
        sum_first(0)
        load_hid.wait()
        for copy in h3:
            copy.wait_recv()
        hm[...] = jnp.zeros_like(hm)
        slots(4, match_hidden)
        until(T_R1[1])
        sum_first(1)
        until(T_R2[0])
        sum_second(0)
        slots(3, lambda j: match_hidden(j + 4))
        until(T_R2[1])
        sum_second(1)
        until(T_P1[0])
        gather_first(0)
        until(T_P1[1])
        gather_first(1)

        gm[...] = jnp.zeros_like(gm)
        GROUP = KB // W

        def match_group(first):
            features = pl.ds(pl.multiple_of(first * W, KB), KB)
            gm[...] += jnp.dot(out[0, :, features], prec[features], preferred_element_type=f32)

        def first_chunk(own_side, s, half):
            side, at = (c, a1) if own_side else (1 - c, a2)
            return side * (NCH // 2) + lax.rem(at + 4 - s, 4) * 8 + half * GROUP

        def done_at(first):
            t = lax.rem(first + NZ * depth, NCH)
            other = NZ * (LAYERS - 1 - t // NZ) + lax.rem(t, NZ)
            return jnp.where(t < NZ * depth, jnp.maximum(t, other), t) + GROUP - 1

        cutoff = T_P2[0]

        def early(own_side, half):
            def one(j):
                first = first_chunk(own_side, j, half)

                @pl.when(done_at(first) < cutoff)
                def _():
                    match_group(first)

            if CHAIN and now[0] < NCH:
                slots(4, one)
            else:
                for j in range(4):
                    match_group(first_chunk(own_side, j, half))

        until(T_P2[0])
        late = []
        for half in (0, 1):
            until(T_P2[half])
            gather_second(half)
            if half == 1:
                until(NCH)
            if now[0] < NCH and CHAIN:
                late.append((True, half))
            early(True, half)
            for s in range(4):
                p3[half, s].wait_recv()
            if now[0] < NCH and CHAIN:
                late.append((False, half))
            early(False, half)
        until(NCH)
        for own_side, half in late:
            def finish(j, _, own_side=own_side, half=half):
                first = first_chunk(own_side, j, half)

                @pl.when(done_at(first) >= cutoff)
                def _():
                    match_group(first)

                return 0

            lax.fori_loop(0, 4, finish, 0)
    else:
        load_bas.wait()
        load_hid.wait()
        until(NCH)

    if COL:
        prod = gm[...] * hm[...]
        pos = lax.broadcasted_iota(jnp.int32, (1, 128), 1)
        side = pos // 64
        p2nd = (pos // 16) % 4
        p1st = (pos // 4) % 4
        query = jnp.where(side == 0, p2nd * 2 + p1st // 2, p1st * 2 + p2nd // 2)
        sums = [jnp.sum(prod[s * SEQLEN:(s + 1) * SEQLEN], axis=0, keepdims=True) for s in (0, 1)]
        lane = lax.broadcasted_iota(jnp.int32, (8, 128), 1)
        line = lax.broadcasted_iota(jnp.int32, (8, 128), 0)
        tile = jnp.zeros((8, 128), f32)
        for s in (0, 1):
            for q in range(8):
                one = jnp.sum(jnp.where(query == q, sums[s], 0.0), axis=1, keepdims=True)
                tile = tile + jnp.where(jnp.logical_and(line == s, lane == q), one, 0.0)
        share[z] = tile / (SEQLEN * QLEN)
        zc = [remote(share.at[z], share.at[z], zs.at[s - 1], zr.at[s - 1], onz(s)) for s in range(1, LAYERS)]
        for copy in zc:
            copy.start()
        for copy in sent:
            copy.wait_send()
    if CHAIN:
        @pl.when(z > 0)
        def _():
            sends = pl.ds(0, NCH - NZ)
            remote(down.at[sends], rcv.at[sends], chain_s, chain_r.at[0], onz(LAYERS - 1)).wait_send()

        @pl.when(z < LAYERS - 1)
        def _():
            sends = pl.ds(0, NUP - NZ)
            remote(ups.at[sends], upr.at[sends], up_s, up_r.at[0], onz(1)).wait_send()

        @pl.when(z == LAYERS - 1)
        def _():
            remote(ups, upr, up_s, up_r.at[0], onz(1)).wait_send()

    if COL:
        for copy in zc:
            copy.wait_recv()
        total = share[0]
        for s in range(1, LAYERS):
            total = total + share[s]
        scores[...] = total[0:2, 0:8]
        for copy in zc:
            copy.wait_send()


def column(incoming, hidden, basis, eigvals, query_grads, query_hidden):
    hbm = pl.BlockSpec(memory_space=pltpu.HBM)
    vmem = pl.BlockSpec(memory_space=pltpu.VMEM)
    dma = pltpu.SemaphoreType.DMA
    section, scores = pl.pallas_call(
        kernel,
        out_shape=(
            pltpu.VMEM((1, 128, D), bf16),
            pltpu.VMEM((2, 8), f32),
        ),
        in_specs=[hbm, hbm, hbm, vmem, vmem, vmem],
        out_specs=(vmem, vmem),
        scratch_shapes=[
            pltpu.VMEM((128, D), bf16),
            pltpu.VMEM((NCH, 128, W), bf16),
            pltpu.VMEM((NCH, 128, W), bf16),
            pltpu.VMEM((NUP, 128, W), bf16),
            pltpu.VMEM((NUP, 128, W), bf16),
            pltpu.VMEM((128, F), bf16),
            pltpu.VMEM((D, 128), f32),
            pltpu.VMEM((16, D // 4), bf16),
            pltpu.VMEM((16, F // 4), bf16),
            pltpu.VMEM((64, D // 4), bf16),
            pltpu.VMEM((64, F // 4), bf16),
            pltpu.VMEM((128, D), bf16),
            pltpu.VMEM((128, F), bf16),
            pltpu.VMEM((4, 8, 128), f32),
            pltpu.VMEM((7, 8, 128), f32),
            pltpu.VMEM((4096, 128), bf16),
            pltpu.VMEM((4096, 128), bf16),
            pltpu.VMEM((1024, 128), f32),
            pltpu.VMEM((4096, 128), bf16),
            pltpu.VMEM((3, 1024, 128), bf16),
            pltpu.VMEM((1024, 128), bf16),
            pltpu.VMEM((3, 256, 128), bf16),
            pltpu.VMEM((D, 128), bf16),
            pltpu.VMEM((256, 256), bf16),
            pltpu.VMEM((128, 256), f32),
            pltpu.VMEM((128, 128), f32),
            pltpu.VMEM((128, 128), f32),
            pltpu.VMEM((LAYERS, 8, 128), f32),
            dma((3,)),
            dma,
            dma((NCH,)),
            dma,
            dma((NUP,)),
            dma((72,)),
            dma((72,)),
            dma((LAYERS - 1,)),
            dma((LAYERS - 1,)),
        ],
        compiler_params=pltpu.CompilerParams(
            collective_id=0, has_side_effects=True, vmem_limit_bytes=60 * 1024 * 1024
        ),
    )(incoming, hidden, basis, eigvals, query_grads, query_hidden)
    return section, scores


def solution(mesh):
    in_specs = (
        P("segment", "col", None),
        P("segment", "col", None),
        P("segment", None, "col"),
        P("segment", "col"),
        P("segment", "col", None),
        P("segment", "col", None),
    )
    out_specs = (P("segment", "col", None), P("col", None))
    return jax.shard_map(column, mesh=mesh, in_specs=in_specs, out_specs=out_specs, check_vma=False)
```

```python
import jax
import jax.numpy as jnp
from jax import lax
from jax.experimental import pallas as pl
from jax.experimental.pallas import tpu as pltpu
from jax.sharding import PartitionSpec as P

D = 8192
F = 14336
K = 4096
SEQLEN = 64
QLEN = 16
DAMP = 0.1

LAYERS = 8
W = 128
NCH = D // W
NZ = 8
NUP = NZ * (LAYERS - 1)
S_E, S_G1, S_H1, S_G2, S_H2, S_BIG, S_SMALL, N_S = range(8)
R_E1, R_E2, R_E3, R_G1, R_H1, R_G2, R_G3, R_H2, R_H3 = range(9)
R_PAIR, R_R1, R_R2, R_P1, R_P2, R_P3, N_R = range(9, 23, 2)
T_H1S, T_G1, T_H1, T_G2, T_G3, T_H2, T_H3 = 8, 10, 18, 22, 23, 40, 43
T_R1 = (39, 43)
T_R2 = (45, 48)
T_P1 = (50, 54)
T_P2 = (59, 62)
PER_P = 8
STORES = 4
CHAIN = True
COL = True

f32 = jnp.float32
bf16 = jnp.bfloat16
MESH = pl.DeviceIdType.MESH


def remote(src, dst, ssem, rsem, dev):
    return pltpu.make_async_remote_copy(
        src_ref=src, dst_ref=dst, send_sem=ssem, recv_sem=rsem, device_id=dev, device_id_type=MESH
    )


def split(v):
    hi = v.astype(bf16)
    return hi, (v - hi.astype(f32)).astype(bf16)


def kernel(
    inc, hid, bas, eig, qg, qh,
    out, scores,
    own, down, rcv, ups, upr, fin, hidv, basv, bhl, eigv, qgr, qhr,
    g16, h16, a1g, a1h, qgv, qhv, ebs, ebr,
    part_out, part_in, kept, mine, r1s, r1r, r2s, r2r, prec,
    wmat, accp, gm, hm, share,
    ld_sem, out_sem, chain_s, chain_r, up_s, up_r, cs, cr, zs, zr,
):
    z = lax.axis_index("segment")
    col = lax.axis_index("col")
    c = lax.rem(col, 2)
    x = lax.rem(col // 2, 4)
    y = col // 8
    a1 = x + c * (y - x)
    a2 = y + c * (x - y)
    step1 = 2 + 6 * c
    step2 = 8 - 6 * c
    depth = LAYERS - 1 - z

    def on1(s):
        return (z, col + (lax.rem(a1 + s, 4) - a1) * step1)

    def on2(s):
        return (z, col + (lax.rem(a2 + s, 4) - a2) * step2)

    def onz(s):
        return (lax.rem(z + s, LAYERS), col)

    sibling = (z, col + 1 - 2 * c)

    barrier = pltpu.get_barrier_semaphore()
    greeted = [sibling] + [on1(s) for s in (1, 2, 3)] + [on2(s) for s in (1, 2, 3)]
    greeted += [onz(s) for s in range(1, LAYERS)]
    for dev in greeted:
        pl.semaphore_signal(barrier, inc=1, device_id=dev, device_id_type=MESH)

    load_own = pltpu.make_async_copy(inc.at[0], own, ld_sem.at[0])
    load_bas = pltpu.make_async_copy(bas.at[0], basv, ld_sem.at[1])
    load_hid = pltpu.make_async_copy(hid.at[0], hidv, ld_sem.at[2])
    small = [
        pltpu.make_async_copy(eig, eigv, ld_sem.at[3]),
        pltpu.make_async_copy(qg, qgr, ld_sem.at[4]),
        pltpu.make_async_copy(qh, qhr, ld_sem.at[5]),
    ]
    for copy in small + [load_own, load_bas, load_hid]:
        copy.start()
    for copy in small:
        copy.wait()

    def fold(q, wide):
        rows = q[0].astype(f32)
        return jnp.concatenate([rows[:, s * wide:(s + 1) * wide] for s in range(4)], axis=0).astype(bf16)

    g16[...] = fold(qgr, D // 4)
    h16[...] = fold(qhr, F // 4)
    ebs[0] = jnp.broadcast_to(eigv[...], (8, 128))
    pl.semaphore_wait(barrier, len(greeted))

    def post(src, dst, dev, send, recv):
        copy = remote(src, dst, cs.at[send], cr.at[recv], dev)
        copy.start()

    def arrived(like, recv):
        remote(like, like, cs.at[0], cr.at[recv], sibling).wait_recv()

    def link(i, t):
        return remote(down.at[i], rcv.at[i], chain_s, chain_r.at[t], onz(LAYERS - 1))

    def uplink(n):
        return remote(ups.at[pl.ds(n, 2)], upr.at[pl.ds(n, 2)], up_s, up_r.at[n // 2], onz(1))

    def lanes(i):
        return pl.ds(pl.multiple_of(i * W, W), W)

    def add(p, q):
        return (p.astype(f32) + q.astype(f32)).astype(bf16)

    def finish_chunk(i, value):
        fin[:, lanes(i)] = value
        pltpu.make_async_copy(fin.at[:, lanes(i)], out.at[0, :, lanes(i)], out_sem).start()

    def chunk_at(t):
        return lax.rem(t + NCH - NZ * depth, NCH)

    def chain_step(t):
        i = chunk_at(t)
        fed = jnp.logical_and(z < LAYERS - 1, t >= NZ)

        @pl.when(fed)
        def _():
            link(i, t - NZ).wait_recv()
            down[i] = add(own[:, lanes(i)], rcv[i])

        @pl.when(jnp.logical_not(fed))
        def _():
            down[i] = own[:, lanes(i)]

        @pl.when(jnp.logical_and(z > 0, t < NCH - NZ))
        def _():
            link(i, t).start()

        partial = t < NZ * depth

        @pl.when(jnp.logical_not(partial))
        def _():
            finish_chunk(i, down[i])

        @pl.when(jnp.logical_and(partial, t // NZ >= LAYERS // 2))
        def _():
            finish_chunk(i, add(down[i], upr[i - (NCH - NUP)]))

    def up_step(t):
        hop = t // NZ
        cut = lax.rem(z - hop + LAYERS, LAYERS)

        @pl.when(jnp.logical_and(cut > 0, lax.rem(t, 2) == 0))
        def _():
            n = (cut - 1) * NZ + t - hop * NZ
            i = NCH - NUP + n
            last = hop == LAYERS - 1
            two = pl.ds(n, 2)

            @pl.when(hop > 0)
            def _():
                uplink(n).wait_recv()

            @pl.when(jnp.logical_and(z >= cut, hop > 0))
            def _():
                for k in (0, 1):
                    ups[n + k] = add(own[:, lanes(i + k)], upr[n + k])

            @pl.when(jnp.logical_and(z >= cut, hop == 0))
            def _():
                for k in (0, 1):
                    ups[n + k] = own[:, lanes(i + k)]

            @pl.when(jnp.logical_and(z < cut, jnp.logical_not(last)))
            def _():
                ups[two] = upr[two]

            @pl.when(jnp.logical_not(last))
            def _():
                uplink(n).start()

            @pl.when(jnp.logical_and(z < cut, cut - z <= LAYERS // 2))
            def _():
                for k in (0, 1):
                    finish_chunk(i + k, add(down[i + k], upr[n + k]))

    now = [0]

    def slots(n, fn=None):
        if not CHAIN:
            now[0] = max(now[0], min(now[0] + n, NCH))
            if fn is not None:
                def plain(j, _):
                    fn(j)
                    return 0

                lax.fori_loop(0, n, plain, 0)
            return
        done = 0
        while done < n:
            base = now[0]
            stop = n - done
            if base < NZ * LAYERS:
                stop = min(stop, NZ * LAYERS - base)
            elif base < NCH:
                stop = min(stop, NCH - base)
            elif fn is None:
                return

            def step(j, _, base=base, done=done):
                if base < NCH:
                    chain_step(base + j)
                if base < NZ * LAYERS:
                    up_step(base + j)
                if fn is not None:
                    fn(done + j)
                return 0

            lax.fori_loop(0, stop, step, 0)
            now[0] += stop
            done += stop

    def until(t):
        if now[0] < t:
            slots(t - now[0])

    if COL:
        for s in (1, 2, 3):
            post(ebs.at[0], ebr.at[s - 1], on1(s), S_E, R_E1)
        for s in (2, 1, 3):
            post(g16, a1g.at[pl.ds(a1 * 16, 16)], on1(s), S_G1, R_G1)

    load_own.wait()

    def order16():
        r = lax.broadcasted_iota(jnp.int32, (64, 64), 0)
        k = lax.broadcasted_iota(jnp.int32, (64, 64), 1)
        src = ((r % 16) // 4) * 16 + (r // 16) * 4 + r % 4
        return (k == src).astype(f32).astype(bf16)

    def rows16(s):
        return pl.ds(pl.multiple_of(c * 64 + lax.rem(a2 + 4 - s, 4) * 16, 16), 16)

    def assemble(a, q, wide):
        part = jnp.dot(order16(), a[...], preferred_element_type=f32).astype(bf16)
        for s in range(4):
            q[rows16(0), s * wide:(s + 1) * wide] = part[s * 16:(s + 1) * 16]

    def share_rows(q, s, dev, send, recv):
        post(q.at[rows16(s)], q.at[rows16(s)], dev, send, recv)

    if COL:
        a1g[pl.ds(pl.multiple_of(a1 * 16, 16), 16)] = g16[...]
        a1h[pl.ds(pl.multiple_of(a1 * 16, 16), 16)] = h16[...]
        until(T_H1S)
        for s in (2, 1, 3):
            post(h16, a1h.at[pl.ds(a1 * 16, 16)], on1(s), S_H1, R_H1)
        until(T_G1)
        arrived(ebr.at[0:3], R_E1)
        ebs[1] = ebs[0] + ebr[0] + ebr[1] + ebr[2]
        for s in (1, 2, 3):
            post(ebs.at[1], ebr.at[2 + s], on2(s), S_E, R_E2)
        arrived(a1g.at[0:48], R_G1)
        assemble(a1g, qgv, D // 4)
        for s in (2, 1, 3):
            share_rows(qgv, 0, on2(s), S_G2, R_G2)
        share_rows(qgv, 0, sibling, S_G2, R_G3)

        KB = 512
        load_bas.wait()

        def split_basis(j):
            for k in (0, 1):
                at = pl.ds(pl.multiple_of((2 * j + k) * KB, KB), KB)
                hi, lo = split(basv[at])
                bhl[at, 0:128] = hi
                bhl[at, 128:256] = lo

        slots(8, split_basis)
        until(T_H1)
        arrived(a1h.at[0:48], R_H1)
        assemble(a1h, qhv, F // 4)
        for s in (2, 1, 3):
            share_rows(qhv, 0, on2(s), S_H2, R_H2)
        share_rows(qhv, 0, sibling, S_H2, R_H3)
        arrived(ebr.at[3:6], R_E2)
        ebs[2] = ebs[1] + ebr[3] + ebr[4] + ebr[5]
        post(ebs.at[2], ebr.at[6], sibling, S_E, R_E3)
        until(T_G2)
        arrived(qgv.at[0:48], R_G2)
        for s in (1, 2, 3):
            share_rows(qgv, s, sibling, S_G2, R_G3)
        until(T_G3)
        arrived(qgv.at[0:64], R_G3)
        arrived(ebr.at[6:7], R_E3)
        ebs[3] = ebs[2] + ebr[6]

        accp[...] = jnp.zeros_like(accp)

        def project(j):
            for k in range(PER_P):
                at = pl.ds(pl.multiple_of((PER_P * j + k) * KB, KB), KB)
                accp[...] += jnp.dot(qgv[:, at], bhl[at], preferred_element_type=f32)

        slots(D // KB // PER_P, project)
        damping = DAMP * jnp.sum(ebs[3][0:1], axis=1, keepdims=True) / K
        weighted = (accp[:, :128] + accp[:, 128:]) / (eigv[...] + damping)
        hi, lo = split(weighted.T)
        wmat[0:128, 0:128] = hi
        wmat[128:256, 0:128] = hi
        wmat[0:128, 128:256] = lo
        wmat[128:256, 128:256] = jnp.zeros_like(lo)

        def expand(side, half):
            at = pl.ds(pl.multiple_of(side * 4096 + half * 2048, 2048), 2048)
            both = jnp.dot(bhl[at], wmat[...], preferred_element_type=f32)
            return both[:, :128] + both[:, 128:]

        def block_rows(block, half):
            return pl.ds(pl.multiple_of(half * 2048 + block * KB, KB), KB)

        def give(half):
            at = pl.ds(half * 2048, 2048)
            part_out[at] = expand(1 - c, half).astype(bf16)
            post(part_out.at[at], part_in.at[at], sibling, S_BIG, R_PAIR + half)

        def keep(half):
            kept[...] = expand(c, half)
            arrived(part_in.at[0:2048], R_PAIR + half)
            for s in (2, 1, 3, 0):
                block = lax.rem(a1 + s, 4)
                at = block_rows(block, half)
                total = kept[pl.ds(pl.multiple_of(block * KB, KB), KB)] + part_in[at].astype(f32)
                if s:
                    r1s[at] = total.astype(bf16)
                    post(r1s.at[at], r1r.at[s - 1, pl.ds(half * KB, KB)], on1(s), S_BIG, R_R1 + half)
                else:
                    mine[pl.ds(half * KB, KB)] = total

        give(0)
        slots(1)
        give(1)
        keep(0)
        slots(1)
        keep(1)

        def match_hidden(j):
            for k in range(4):
                at = pl.ds(pl.multiple_of((4 * j + k) * 512, 512), 512)
                hm[...] += lax.dot_general(
                    hidv[:, at], qhv[:, at], (((1,), (1,)), ((), ())), preferred_element_type=f32
                )

        def sum_first(half):
            arrived(prec.at[0:3 * KB], R_R1 + half)
            for s in (2, 1, 3, 0):
                at = pl.ds(pl.multiple_of(half * KB + lax.rem(a2 + s, 4) * 128, 128), 128)
                total = mine[at] + r1r[0, at].astype(f32) + r1r[1, at].astype(f32) + r1r[2, at].astype(f32)
                if s:
                    r2s[at] = total.astype(bf16)
                    post(r2s.at[at], r2r.at[s - 1, pl.ds(half * 128, 128)], on2(s), S_SMALL, R_R2 + half)
                else:
                    mine[at] = total

        def sum_second(half):
            arrived(prec.at[0:384], R_R2 + half)
            at = pl.ds(pl.multiple_of(half * KB + a2 * 128, 128), 128)
            got = pl.ds(half * 128, 128)
            total = mine[at] + r2r[0, got].astype(f32) + r2r[1, got].astype(f32) + r2r[2, got].astype(f32)
            rows = pl.ds(pl.multiple_of(c * 4096 + half * 2048 + a1 * KB + a2 * 128, 128), 128)
            prec[rows] = total.astype(bf16)
            for s in (2, 1, 3):
                post(prec.at[rows], prec.at[rows], on2(s), S_SMALL, R_P1 + half)

        def band(s, half):
            return pl.ds(pl.multiple_of(c * 4096 + half * 2048 + lax.rem(a1 + 4 - s, 4) * KB, KB), KB)

        def gather_first(half):
            arrived(prec.at[0:384], R_P1 + half)
            rows = band(0, half)
            for s in (2, 1, 3):
                post(prec.at[rows], prec.at[rows], on1(s), S_BIG, R_P2 + half)
            post(prec.at[rows], prec.at[rows], sibling, S_BIG, R_P3 + half)

        def gather_second(half):
            arrived(prec.at[0:3 * KB], R_P2 + half)
            for s in (1, 2, 3):
                rows = band(s, half)
                post(prec.at[rows], prec.at[rows], sibling, S_BIG, R_P3 + half)

        until(T_R1[0])
        sum_first(0)
        until(T_H2)
        arrived(qhv.at[0:48], R_H2)
        for s in (1, 2, 3):
            share_rows(qhv, s, sibling, S_H2, R_H3)
        until(T_R1[1])
        sum_first(1)
        until(T_H3)
        load_hid.wait()
        arrived(qhv.at[0:64], R_H3)
        hm[...] = jnp.zeros_like(hm)
        slots(2, match_hidden)
        until(T_R2[0])
        sum_second(0)
        slots(2, lambda j: match_hidden(j + 2))
        until(T_R2[1])
        sum_second(1)
        slots(2, lambda j: match_hidden(j + 4))
        until(T_P1[0])
        gather_first(0)
        slots(1, lambda j: match_hidden(j + 6))
        until(T_P1[1])
        gather_first(1)

        gm[...] = jnp.zeros_like(gm)
        GROUP = KB // W

        def match_group(first):
            features = pl.ds(pl.multiple_of(first * W, KB), KB)
            gm[...] += jnp.dot(fin[:, features], prec[features], preferred_element_type=f32)

        def first_chunk(own_side, s, half):
            side, at = (c, a1) if own_side else (1 - c, a2)
            return side * (NCH // 2) + half * (NCH // 4) + lax.rem(at + 4 - s, 4) * GROUP

        def done_at(first):
            t = lax.rem(first + NZ * depth, NCH)
            other = NZ * (LAYERS - 1 - t // NZ) + lax.rem(t, NZ)
            return jnp.where(t < NZ * depth, jnp.maximum(t, other), t) + GROUP - 1

        cutoff = T_P2[0]

        def early(own_side, half):
            def one(j):
                first = first_chunk(own_side, j, half)

                @pl.when(done_at(first) < cutoff)
                def _():
                    match_group(first)

            if CHAIN and now[0] < NCH:
                slots(4, one)
            else:
                for j in range(4):
                    match_group(first_chunk(own_side, j, half))

        until(T_P2[0])
        late = []
        for half in (0, 1):
            until(T_P2[half])
            gather_second(half)
            if half == 1:
                until(NCH)
            if now[0] < NCH and CHAIN:
                late.append((True, half))
            early(True, half)
            arrived(prec.at[0:2048], R_P3 + half)
            if now[0] < NCH and CHAIN:
                late.append((False, half))
            early(False, half)
        until(NCH)
        for own_side, half in late:
            for j in range(4):
                first = first_chunk(own_side, j, half)

                @pl.when(done_at(first) >= cutoff)
                def _(first=first):
                    match_group(first)
    else:
        load_bas.wait()
        load_hid.wait()
        until(NCH)

    if COL:
        prod = gm[...] * hm[...]
        pos = lax.broadcasted_iota(jnp.int32, (128, 128), 0)
        side = pos // 64
        p2nd = (pos // 16) % 4
        p1st = (pos // 4) % 4
        query = jnp.where(side == 0, p2nd * 2 + p1st // 2, p1st * 2 + p2nd // 2)
        pick = (query == lax.broadcasted_iota(jnp.int32, (128, 128), 1)).astype(f32)
        sums = [jnp.sum(prod[s * SEQLEN:(s + 1) * SEQLEN], axis=0, keepdims=True) for s in (0, 1)]
        line = lax.broadcasted_iota(jnp.int32, (8, 128), 0)
        both = jnp.where(line == 0, sums[0], jnp.where(line == 1, sums[1], 0.0))
        tile = jnp.dot(both, pick, precision=lax.Precision.HIGHEST, preferred_element_type=f32)
        share[z] = tile / (SEQLEN * QLEN)
        for s in (4, 3, 5, 2, 6, 1, 7):
            remote(share.at[z], share.at[z], zs, zr, onz(s)).start()
        for like, kind in (
            (ebr, S_E),
            (a1g.at[0:48], S_G1),
            (a1h.at[0:48], S_H1),
            (qgv.at[0:112], S_G2),
            (qhv.at[0:112], S_H2),
            (bhl.at[0:7168], S_BIG),
            (prec.at[0:1536], S_SMALL),
        ):
            remote(like, like, cs.at[kind], cr.at[0], sibling).wait_send()
    if CHAIN:
        pltpu.make_async_copy(fin, out.at[0], out_sem).wait()

        @pl.when(z > 0)
        def _():
            sends = pl.ds(0, NCH - NZ)
            remote(down.at[sends], rcv.at[sends], chain_s, chain_r.at[0], onz(LAYERS - 1)).wait_send()

        @pl.when(z < LAYERS - 1)
        def _():
            sends = pl.ds(0, NUP - NZ)
            remote(ups.at[sends], upr.at[sends], up_s, up_r.at[0], onz(1)).wait_send()

        @pl.when(z == LAYERS - 1)
        def _():
            remote(ups, upr, up_s, up_r.at[0], onz(1)).wait_send()

    if COL:
        others = remote(share.at[0:LAYERS - 1], share.at[0:LAYERS - 1], zs, zr, sibling)
        others.wait_recv()
        total = share[0]
        for s in range(1, LAYERS):
            total = total + share[s]
        scores[...] = total[0:2, 0:8]
        others.wait_send()


def store(section, scores, section_out, scores_out, sem):
    rows = 128 // STORES
    copies = [
        pltpu.make_async_copy(section.at[0, pl.ds(k * rows, rows)], section_out.at[0, pl.ds(k * rows, rows)], sem.at[k])
        for k in range(STORES)
    ]
    copies.append(pltpu.make_async_copy(scores, scores_out, sem.at[STORES]))
    for copy in copies:
        copy.start()
    for copy in copies:
        copy.wait()


def column(incoming, hidden, basis, eigvals, query_grads, query_hidden):
    hbm = pl.BlockSpec(memory_space=pltpu.HBM)
    vmem = pl.BlockSpec(memory_space=pltpu.VMEM)
    dma = pltpu.SemaphoreType.DMA
    section, scores = pl.pallas_call(
        kernel,
        out_shape=(
            pltpu.VMEM((1, 128, D), bf16),
            pltpu.VMEM((2, 8), f32),
        ),
        in_specs=[hbm] * 6,
        out_specs=(pl.BlockSpec(memory_space=pl.ANY), vmem),
        scratch_shapes=[
            pltpu.VMEM((128, D), bf16),
            pltpu.VMEM((NCH, 128, W), bf16),
            pltpu.VMEM((NCH, 128, W), bf16),
            pltpu.VMEM((NUP, 128, W), bf16),
            pltpu.VMEM((NUP, 128, W), bf16),
            pltpu.VMEM((128, D), bf16),
            pltpu.VMEM((128, F), bf16),
            pltpu.VMEM((D, 128), f32),
            pltpu.VMEM((D, 256), bf16),
            pltpu.VMEM((1, 128), f32),
            pltpu.VMEM((1, 4, D), bf16),
            pltpu.VMEM((1, 4, F), bf16),
            pltpu.VMEM((16, D // 4), bf16),
            pltpu.VMEM((16, F // 4), bf16),
            pltpu.VMEM((64, D // 4), bf16),
            pltpu.VMEM((64, F // 4), bf16),
            pltpu.VMEM((128, D), bf16),
            pltpu.VMEM((128, F), bf16),
            pltpu.VMEM((4, 8, 128), f32),
            pltpu.VMEM((7, 8, 128), f32),
            pltpu.VMEM((4096, 128), bf16),
            pltpu.VMEM((4096, 128), bf16),
            pltpu.VMEM((2048, 128), f32),
            pltpu.VMEM((1024, 128), f32),
            pltpu.VMEM((4096, 128), bf16),
            pltpu.VMEM((3, 1024, 128), bf16),
            pltpu.VMEM((1024, 128), bf16),
            pltpu.VMEM((3, 256, 128), bf16),
            pltpu.VMEM((D, 128), bf16),
            pltpu.VMEM((256, 256), bf16),
            pltpu.VMEM((128, 256), f32),
            pltpu.VMEM((128, 128), f32),
            pltpu.VMEM((128, 128), f32),
            pltpu.VMEM((LAYERS, 8, 128), f32),
            dma((6,)),
            dma,
            dma,
            dma((NCH - NZ,)),
            dma,
            dma((NUP // 2,)),
            dma((N_S,)),
            dma((N_R,)),
            dma,
            dma,
        ],
        compiler_params=pltpu.CompilerParams(
            collective_id=0, has_side_effects=True, vmem_limit_bytes=60 * 1024 * 1024
        ),
    )(incoming, hidden, basis, eigvals, query_grads, query_hidden)
    anyspace = pl.BlockSpec(memory_space=pl.ANY)
    return pl.pallas_call(
        store,
        out_shape=(
            jax.ShapeDtypeStruct((1, 128, D), bf16),
            jax.ShapeDtypeStruct((2, 8), f32),
        ),
        in_specs=[anyspace, anyspace],
        out_specs=(hbm, hbm),
        scratch_shapes=[dma((STORES + 1,))],
        compiler_params=pltpu.CompilerParams(vmem_limit_bytes=1024 * 1024),
    )(section, scores)


def solution(mesh):
    in_specs = (
        P("segment", "col", None),
        P("segment", "col", None),
        P("segment", None, "col"),
        P("segment", "col"),
        P("segment", "col", None),
        P("segment", "col", None),
    )
    out_specs = (P("segment", "col", None), P("col", None))
    return jax.shard_map(column, mesh=mesh, in_specs=in_specs, out_specs=out_specs, check_vma=False)
```

```python
import jax
import jax.numpy as jnp
from jax import lax
from jax.experimental import pallas as pl
from jax.experimental.pallas import tpu as pltpu
from jax.sharding import PartitionSpec as P

D = 8192
F = 14336
K = 4096
SEQLEN = 64
QLEN = 16
DAMP = 0.1

LAYERS = 8
W = 256
NCH = D // W
NZ = 4
NUP = NZ * (LAYERS - 1)
S_E, S_G1, S_H1, S_G2, S_H2, S_BIG, S_SMALL, N_S = range(8)
R_E1, R_E2, R_E3, R_G1, R_H1, R_H2, R_H3 = range(7)
R_G2, R_G3, R_PAIR, R_R1, R_R2, R_P1, R_P2, R_P3, N_R = range(7, 25, 2)
SLOTS = 2 * NCH
T_H1S, T_G1, T_H1, T_H2, T_H3 = 8, 10, 18, 43, 51
T_G2 = (17, 21)
T_G3 = (19, 23)
T_R1 = (38, 42)
T_R2 = (45, 48)
T_P1 = (49, 51)
T_P2 = (57, 60)
PER_P = 8
KB = 512
HALF = D // 2
STORES = 4
CHAIN = True
COL = True

f32 = jnp.float32
bf16 = jnp.bfloat16
MESH = pl.DeviceIdType.MESH


def remote(src, dst, ssem, rsem, dev):
    return pltpu.make_async_remote_copy(
        src_ref=src, dst_ref=dst, send_sem=ssem, recv_sem=rsem, device_id=dev, device_id_type=MESH
    )


def split(v):
    hi = v.astype(bf16)
    return hi, (v - hi.astype(f32)).astype(bf16)


def kernel(
    inc, hid, bas, eig, qg, qh,
    out, scores,
    own, down, rcv, ups, upr, fin, hidv, basv, bhl, eigv, qgr, qhr,
    g16, h16, a1g, a1h, qgv, qhv, ebs, ebr,
    part_out, part_in, kept, mine, r1s, r1r, r2s, r2r, prec,
    wmat, accp, gm, hm, share,
    ld_sem, out_sem, chain_s, chain_r, up_s, up_r, cs, cr, zs, zr,
):
    z = lax.axis_index("segment")
    col = lax.axis_index("col")
    c = lax.rem(col, 2)
    x = lax.rem(col // 2, 4)
    y = col // 8
    a1 = x + c * (y - x)
    a2 = y + c * (x - y)
    step1 = 2 + 6 * c
    step2 = 8 - 6 * c
    depth = LAYERS - 1 - z

    def on1(s):
        return (z, col + (lax.rem(a1 + s, 4) - a1) * step1)

    def on2(s):
        return (z, col + (lax.rem(a2 + s, 4) - a2) * step2)

    def onz(s):
        return (lax.rem(z + s, LAYERS), col)

    sibling = (z, col + 1 - 2 * c)

    barrier = pltpu.get_barrier_semaphore()
    greeted = [sibling] + [on1(s) for s in (1, 2, 3)] + [on2(s) for s in (1, 2, 3)]
    greeted += [onz(s) for s in range(1, LAYERS)]
    for dev in greeted:
        pl.semaphore_signal(barrier, inc=1, device_id=dev, device_id_type=MESH)

    load_own = pltpu.make_async_copy(inc.at[0], own, ld_sem.at[0])
    load_bas = pltpu.make_async_copy(bas.at[0], basv, ld_sem.at[1])
    load_hid = pltpu.make_async_copy(hid.at[0], hidv, ld_sem.at[2])
    small = [
        pltpu.make_async_copy(eig, eigv, ld_sem.at[3]),
        pltpu.make_async_copy(qg, qgr, ld_sem.at[4]),
        pltpu.make_async_copy(qh, qhr, ld_sem.at[5]),
    ]
    for copy in small + [load_own, load_bas, load_hid]:
        copy.start()
    for copy in small:
        copy.wait()

    def fold(q, wide):
        rows = q[0].astype(f32)
        return jnp.concatenate([rows[:, s * wide:(s + 1) * wide] for s in range(4)], axis=0).astype(bf16)

    g16[...] = fold(qgr, D // 4)
    h16[...] = fold(qhr, F // 4)
    ebs[0] = jnp.broadcast_to(eigv[...], (8, 128))
    pl.semaphore_wait(barrier, len(greeted))

    def post(src, dst, dev, send, recv):
        copy = remote(src, dst, cs.at[send], cr.at[recv], dev)
        copy.start()

    def arrived(like, recv):
        remote(like, like, cs.at[0], cr.at[recv], sibling).wait_recv()

    def link(i, t):
        return remote(down.at[i], rcv.at[i], chain_s, chain_r.at[t], onz(LAYERS - 1))

    def uplink(n):
        return remote(ups.at[n], upr.at[n], up_s, up_r.at[n], onz(1))

    def lanes(i):
        return pl.ds(pl.multiple_of(i * W, W), W)

    def add(p, q):
        return (p.astype(f32) + q.astype(f32)).astype(bf16)

    def finish_chunk(i, value):
        fin[:, lanes(i)] = value
        pltpu.make_async_copy(fin.at[:, lanes(i)], out.at[0, :, lanes(i)], out_sem).start()

    def chunk_at(t):
        return lax.rem(t + NCH - NZ * depth, NCH)

    def chain_step(t):
        i = chunk_at(t)
        fed = jnp.logical_and(z < LAYERS - 1, t >= NZ)

        @pl.when(fed)
        def _():
            link(i, t - NZ).wait_recv()
            down[i] = add(own[:, lanes(i)], rcv[i])

        @pl.when(jnp.logical_not(fed))
        def _():
            down[i] = own[:, lanes(i)]

        @pl.when(jnp.logical_and(z > 0, t < NCH - NZ))
        def _():
            link(i, t).start()

        partial = t < NZ * depth

        @pl.when(jnp.logical_not(partial))
        def _():
            finish_chunk(i, down[i])

        @pl.when(jnp.logical_and(partial, t // NZ >= LAYERS // 2))
        def _():
            finish_chunk(i, add(down[i], upr[i - (NCH - NUP)]))

    def up_step(t):
        hop = t // NZ
        cut = lax.rem(z - hop + LAYERS, LAYERS)

        @pl.when(cut > 0)
        def _():
            n = (cut - 1) * NZ + t - hop * NZ
            i = NCH - NUP + n
            last = hop == LAYERS - 1

            @pl.when(hop > 0)
            def _():
                uplink(n).wait_recv()

            @pl.when(jnp.logical_and(z >= cut, hop > 0))
            def _():
                ups[n] = add(own[:, lanes(i)], upr[n])

            @pl.when(jnp.logical_and(z >= cut, hop == 0))
            def _():
                ups[n] = own[:, lanes(i)]

            @pl.when(jnp.logical_and(z < cut, jnp.logical_not(last)))
            def _():
                ups[n] = upr[n]

            @pl.when(jnp.logical_not(last))
            def _():
                uplink(n).start()

            @pl.when(jnp.logical_and(z < cut, cut - z <= LAYERS // 2))
            def _():
                finish_chunk(i, add(down[i], upr[n]))

    now = [0]

    def slots(n, fn=None):
        if CHAIN:
            ahead = min(n, SLOTS - now[0])
        else:
            ahead = 0
        base = now[0]

        def step(j, _):
            t = base + j

            @pl.when(lax.rem(t, 2) == 0)
            def _():
                chain_step(t // 2)

            @pl.when(lax.rem(t, 2) == 1)
            def _():
                up_step(t // 2)

            if fn is not None:
                fn(j)
            return 0

        if ahead:
            lax.fori_loop(0, ahead, step, 0)
        if fn is not None and n > ahead:
            lax.fori_loop(ahead, n, lambda j, _: (fn(j), 0)[1], 0)
        now[0] = min(base + n, SLOTS)

    def until(t):
        if now[0] < t:
            slots(t - now[0])

    if COL:
        for s in (1, 2, 3):
            post(ebs.at[0], ebr.at[s - 1], on1(s), S_E, R_E1)
        for s in (2, 1, 3):
            post(g16, a1g.at[pl.ds(a1 * 16, 16)], on1(s), S_G1, R_G1)

    load_own.wait()

    def order16():
        r = lax.broadcasted_iota(jnp.int32, (64, 64), 0)
        k = lax.broadcasted_iota(jnp.int32, (64, 64), 1)
        src = ((r % 16) // 4) * 16 + (r // 16) * 4 + r % 4
        return (k == src).astype(f32).astype(bf16)

    def rows16(s):
        return pl.ds(pl.multiple_of(c * 64 + lax.rem(a2 + 4 - s, 4) * 16, 16), 16)

    def assemble(a, q, wide):
        part = jnp.dot(order16(), a[...], preferred_element_type=f32).astype(bf16)
        for s in range(4):
            q[rows16(0), s * wide:(s + 1) * wide] = part[s * 16:(s + 1) * 16]

    def share_rows(q, s, dev, send, recv):
        post(q.at[rows16(s)], q.at[rows16(s)], dev, send, recv)

    def share_half(s, half, dev, recv):
        part = qgv.at[rows16(s), half * HALF:(half + 1) * HALF]
        post(part, part, dev, S_G2, recv + half)

    if COL:
        a1g[pl.ds(pl.multiple_of(a1 * 16, 16), 16)] = g16[...]
        a1h[pl.ds(pl.multiple_of(a1 * 16, 16), 16)] = h16[...]
        until(T_H1S)
        for s in (2, 1, 3):
            post(h16, a1h.at[pl.ds(a1 * 16, 16)], on1(s), S_H1, R_H1)
        until(T_G1)
        arrived(ebr.at[0:3], R_E1)
        ebs[1] = ebs[0] + ebr[0] + ebr[1] + ebr[2]
        for s in (1, 2, 3):
            post(ebs.at[1], ebr.at[2 + s], on2(s), S_E, R_E2)
        arrived(a1g.at[0:48], R_G1)
        assemble(a1g, qgv, D // 4)
        for half in (0, 1):
            for s in (2, 1, 3):
                share_half(0, half, on2(s), R_G2)
        for half in (0, 1):
            share_half(0, half, sibling, R_G3)

        load_bas.wait()

        def split_basis(j):
            for k in (0, 1):
                at = pl.ds(pl.multiple_of((2 * j + k) * KB, KB), KB)
                hi, lo = split(basv[at])
                bhl[at, 0:128] = hi
                bhl[at, 128:256] = lo

        accp[...] = jnp.zeros_like(accp)

        def project(half):
            arrived(qgv.at[0:64, 0:HALF], R_G3 + half)

            def blocks(j):
                for k in range(PER_P):
                    at = pl.ds(pl.multiple_of(half * HALF + (PER_P * j + k) * KB, KB), KB)
                    accp[...] += jnp.dot(qgv[:, at], bhl[at], preferred_element_type=f32)

            slots(HALF // KB // PER_P, blocks)

        def swap_half(half):
            arrived(qgv.at[0:48, 0:HALF], R_G2 + half)
            for s in (1, 2, 3):
                share_half(s, half, sibling, R_G3)

        slots(7, split_basis)
        until(T_G2[0])
        swap_half(0)
        until(T_H1)
        arrived(a1h.at[0:48], R_H1)
        assemble(a1h, qhv, F // 4)
        for s in (2, 1, 3):
            share_rows(qhv, 0, on2(s), S_H2, R_H2)
        share_rows(qhv, 0, sibling, S_H2, R_H3)
        split_basis(7)
        arrived(ebr.at[3:6], R_E2)
        ebs[2] = ebs[1] + ebr[3] + ebr[4] + ebr[5]
        post(ebs.at[2], ebr.at[6], sibling, S_E, R_E3)
        until(T_G3[0])
        project(0)
        until(T_G2[1])
        swap_half(1)
        until(T_G3[1])
        arrived(ebr.at[6:7], R_E3)
        ebs[3] = ebs[2] + ebr[6]
        project(1)
        damping = DAMP * jnp.sum(ebs[3][0:1], axis=1, keepdims=True) / K
        weighted = (accp[:, :128] + accp[:, 128:]) / (eigv[...] + damping)
        hi, lo = split(weighted.T)
        wmat[0:128, 0:128] = hi
        wmat[128:256, 0:128] = hi
        wmat[0:128, 128:256] = lo
        wmat[128:256, 128:256] = jnp.zeros_like(lo)

        def expand(side, half):
            at = pl.ds(pl.multiple_of(side * 4096 + half * 2048, 2048), 2048)
            both = jnp.dot(bhl[at], wmat[...], preferred_element_type=f32)
            return both[:, :128] + both[:, 128:]

        def block_rows(block, half):
            return pl.ds(pl.multiple_of(half * 2048 + block * KB, KB), KB)

        def give(half):
            at = pl.ds(half * 2048, 2048)
            part_out[at] = expand(1 - c, half).astype(bf16)
            post(part_out.at[at], part_in.at[at], sibling, S_BIG, R_PAIR + half)

        def keep(half):
            kept[pl.ds(half * 2048, 2048)] = expand(c, half)

        def add_pair(half):
            arrived(part_in.at[0:2048], R_PAIR + half)
            for s in (2, 1, 3, 0):
                at = block_rows(lax.rem(a1 + s, 4), half)
                total = kept[at] + part_in[at].astype(f32)
                if s:
                    r1s[at] = total.astype(bf16)
                    post(r1s.at[at], r1r.at[s - 1, pl.ds(half * KB, KB)], on1(s), S_BIG, R_R1 + half)
                else:
                    mine[pl.ds(half * KB, KB)] = total

        give(0)
        keep(0)
        slots(2)
        give(1)
        add_pair(0)
        slots(2)
        keep(1)
        add_pair(1)

        def match_hidden(j):
            for k in range(4):
                at = pl.ds(pl.multiple_of((4 * j + k) * 512, 512), 512)
                hm[...] += lax.dot_general(
                    hidv[:, at], qhv[:, at], (((1,), (1,)), ((), ())), preferred_element_type=f32
                )

        def sum_first(half):
            arrived(prec.at[0:3 * KB], R_R1 + half)
            for s in (2, 1, 3, 0):
                at = pl.ds(pl.multiple_of(half * KB + lax.rem(a2 + s, 4) * 128, 128), 128)
                total = mine[at] + r1r[0, at].astype(f32) + r1r[1, at].astype(f32) + r1r[2, at].astype(f32)
                if s:
                    r2s[at] = total.astype(bf16)
                    post(r2s.at[at], r2r.at[s - 1, pl.ds(half * 128, 128)], on2(s), S_SMALL, R_R2 + half)
                else:
                    mine[at] = total

        def sum_second(half):
            arrived(prec.at[0:384], R_R2 + half)
            at = pl.ds(pl.multiple_of(half * KB + a2 * 128, 128), 128)
            got = pl.ds(half * 128, 128)
            total = mine[at] + r2r[0, got].astype(f32) + r2r[1, got].astype(f32) + r2r[2, got].astype(f32)
            rows = pl.ds(pl.multiple_of(c * 4096 + half * 2048 + a1 * KB + a2 * 128, 128), 128)
            prec[rows] = total.astype(bf16)
            for s in (2, 1, 3):
                post(prec.at[rows], prec.at[rows], on2(s), S_SMALL, R_P1 + half)

        def band(s, half):
            return pl.ds(pl.multiple_of(c * 4096 + half * 2048 + lax.rem(a1 + 4 - s, 4) * KB, KB), KB)

        def gather_first(half):
            arrived(prec.at[0:384], R_P1 + half)
            rows = band(0, half)
            for s in (2, 1, 3):
                post(prec.at[rows], prec.at[rows], on1(s), S_BIG, R_P2 + half)
            post(prec.at[rows], prec.at[rows], sibling, S_BIG, R_P3 + half)

        def gather_second(half):
            arrived(prec.at[0:3 * KB], R_P2 + half)
            for s in (1, 2, 3):
                rows = band(s, half)
                post(prec.at[rows], prec.at[rows], sibling, S_BIG, R_P3 + half)

        until(T_R1[0])
        sum_first(0)
        until(T_R1[1])
        sum_first(1)
        until(T_H2)
        arrived(qhv.at[0:48], R_H2)
        for s in (1, 2, 3):
            share_rows(qhv, s, sibling, S_H2, R_H3)
        for half in (0, 1):
            until(T_R2[half])
            sum_second(half)
        for half in (0, 1):
            until(T_P1[half])
            gather_first(half)
        until(T_H3)
        load_hid.wait()
        arrived(qhv.at[0:64], R_H3)
        hm[...] = jnp.zeros_like(hm)
        slots(F // 2048, match_hidden)

        gm[...] = jnp.zeros_like(gm)
        GROUP = KB // W

        def match_group(first):
            features = pl.ds(pl.multiple_of(first * W, KB), KB)
            gm[...] += jnp.dot(fin[:, features], prec[features], preferred_element_type=f32)

        def first_chunk(own_side, s, half):
            side, at = (c, a1) if own_side else (1 - c, a2)
            return side * (NCH // 2) + half * (NCH // 4) + lax.rem(at + 4 - s, 4) * GROUP

        def done_at(first):
            t = lax.rem(first + NZ * depth, NCH)
            other = NZ * (LAYERS - 1 - t // NZ) + lax.rem(t, NZ)
            return 2 * (jnp.where(t < NZ * depth, jnp.maximum(t, other), t) + GROUP - 1) + 1

        late = []

        def early(own_side, half):
            seen = now[0]
            if not CHAIN or seen >= SLOTS:
                for j in range(4):
                    match_group(first_chunk(own_side, j, half))
                return

            def two(j):
                for k in (0, 1):
                    first = first_chunk(own_side, 2 * j + k, half)

                    @pl.when(done_at(first) < seen)
                    def _(first=first):
                        match_group(first)

            slots(2, two)
            late.append((own_side, half, seen))

        until(T_P2[0])
        gather_second(0)
        early(True, 0)
        until(T_P2[1])
        gather_second(1)
        arrived(prec.at[0:2048], R_P3)
        early(False, 0)
        until(SLOTS)
        early(True, 1)
        arrived(prec.at[0:2048], R_P3 + 1)
        early(False, 1)
        for own_side, half, seen in late:
            for j in range(4):
                first = first_chunk(own_side, j, half)

                @pl.when(done_at(first) >= seen)
                def _(first=first):
                    match_group(first)
    else:
        load_bas.wait()
        load_hid.wait()
        until(SLOTS)

    if COL:
        prod = gm[...] * hm[...]
        pos = lax.broadcasted_iota(jnp.int32, (128, 128), 0)
        side = pos // 64
        p2nd = (pos // 16) % 4
        p1st = (pos // 4) % 4
        query = jnp.where(side == 0, p2nd * 2 + p1st // 2, p1st * 2 + p2nd // 2)
        pick = (query == lax.broadcasted_iota(jnp.int32, (128, 128), 1)).astype(f32)
        sums = [jnp.sum(prod[s * SEQLEN:(s + 1) * SEQLEN], axis=0, keepdims=True) for s in (0, 1)]
        line = lax.broadcasted_iota(jnp.int32, (8, 128), 0)
        both = jnp.where(line == 0, sums[0], jnp.where(line == 1, sums[1], 0.0))
        tile = jnp.dot(both, pick, precision=lax.Precision.HIGHEST, preferred_element_type=f32)
        share[z] = tile / (SEQLEN * QLEN)
        for s in (4, 3, 5, 2, 6, 1, 7):
            remote(share.at[z], share.at[z], zs, zr, onz(s)).start()
        for like, kind in (
            (ebr, S_E),
            (a1g.at[0:48], S_G1),
            (a1h.at[0:48], S_H1),
            (qgv.at[0:112], S_G2),
            (qhv.at[0:112], S_H2),
            (bhl.at[0:7168], S_BIG),
            (prec.at[0:1536], S_SMALL),
        ):
            remote(like, like, cs.at[kind], cr.at[0], sibling).wait_send()
    if CHAIN:
        pltpu.make_async_copy(fin, out.at[0], out_sem).wait()

        @pl.when(z > 0)
        def _():
            sends = pl.ds(0, NCH - NZ)
            remote(down.at[sends], rcv.at[sends], chain_s, chain_r.at[0], onz(LAYERS - 1)).wait_send()

        @pl.when(z < LAYERS - 1)
        def _():
            sends = pl.ds(0, NUP - NZ)
            remote(ups.at[sends], upr.at[sends], up_s, up_r.at[0], onz(1)).wait_send()

        @pl.when(z == LAYERS - 1)
        def _():
            remote(ups, upr, up_s, up_r.at[0], onz(1)).wait_send()

    if COL:
        others = remote(share.at[0:LAYERS - 1], share.at[0:LAYERS - 1], zs, zr, sibling)
        others.wait_recv()
        total = share[0]
        for s in range(1, LAYERS):
            total = total + share[s]
        scores[...] = total[0:2, 0:8]
        others.wait_send()


def store(section, scores, section_out, scores_out, sem):
    rows = 128 // STORES
    copies = [
        pltpu.make_async_copy(section.at[0, pl.ds(k * rows, rows)], section_out.at[0, pl.ds(k * rows, rows)], sem.at[k])
        for k in range(STORES)
    ]
    copies.append(pltpu.make_async_copy(scores, scores_out, sem.at[STORES]))
    for copy in copies:
        copy.start()
    for copy in copies:
        copy.wait()


def column(incoming, hidden, basis, eigvals, query_grads, query_hidden):
    hbm = pl.BlockSpec(memory_space=pltpu.HBM)
    vmem = pl.BlockSpec(memory_space=pltpu.VMEM)
    dma = pltpu.SemaphoreType.DMA
    section, scores = pl.pallas_call(
        kernel,
        out_shape=(
            pltpu.VMEM((1, 128, D), bf16),
            pltpu.VMEM((2, 8), f32),
        ),
        in_specs=[hbm] * 6,
        out_specs=(pl.BlockSpec(memory_space=pl.ANY), vmem),
        scratch_shapes=[
            pltpu.VMEM((128, D), bf16),
            pltpu.VMEM((NCH, 128, W), bf16),
            pltpu.VMEM((NCH, 128, W), bf16),
            pltpu.VMEM((NUP, 128, W), bf16),
            pltpu.VMEM((NUP, 128, W), bf16),
            pltpu.VMEM((128, D), bf16),
            pltpu.VMEM((128, F), bf16),
            pltpu.VMEM((D, 128), f32),
            pltpu.VMEM((D, 256), bf16),
            pltpu.VMEM((1, 128), f32),
            pltpu.VMEM((1, 4, D), bf16),
            pltpu.VMEM((1, 4, F), bf16),
            pltpu.VMEM((16, D // 4), bf16),
            pltpu.VMEM((16, F // 4), bf16),
            pltpu.VMEM((64, D // 4), bf16),
            pltpu.VMEM((64, F // 4), bf16),
            pltpu.VMEM((128, D), bf16),
            pltpu.VMEM((128, F), bf16),
            pltpu.VMEM((4, 8, 128), f32),
            pltpu.VMEM((7, 8, 128), f32),
            pltpu.VMEM((4096, 128), bf16),
            pltpu.VMEM((4096, 128), bf16),
            pltpu.VMEM((4096, 128), f32),
            pltpu.VMEM((1024, 128), f32),
            pltpu.VMEM((4096, 128), bf16),
            pltpu.VMEM((3, 1024, 128), bf16),
            pltpu.VMEM((1024, 128), bf16),
            pltpu.VMEM((3, 256, 128), bf16),
            pltpu.VMEM((D, 128), bf16),
            pltpu.VMEM((256, 256), bf16),
            pltpu.VMEM((128, 256), f32),
            pltpu.VMEM((128, 128), f32),
            pltpu.VMEM((128, 128), f32),
            pltpu.VMEM((LAYERS, 8, 128), f32),
            dma((6,)),
            dma,
            dma,
            dma((NCH - NZ,)),
            dma,
            dma((NUP,)),
            dma((N_S,)),
            dma((N_R,)),
            dma,
            dma,
        ],
        compiler_params=pltpu.CompilerParams(
            collective_id=0, has_side_effects=True, vmem_limit_bytes=60 * 1024 * 1024
        ),
    )(incoming, hidden, basis, eigvals, query_grads, query_hidden)
    anyspace = pl.BlockSpec(memory_space=pl.ANY)
    return pl.pallas_call(
        store,
        out_shape=(
            jax.ShapeDtypeStruct((1, 128, D), bf16),
            jax.ShapeDtypeStruct((2, 8), f32),
        ),
        in_specs=[anyspace, anyspace],
        out_specs=(hbm, hbm),
        scratch_shapes=[dma((STORES + 1,))],
        compiler_params=pltpu.CompilerParams(vmem_limit_bytes=1024 * 1024),
    )(section, scores)


def solution(mesh):
    in_specs = (
        P("segment", "col", None),
        P("segment", "col", None),
        P("segment", None, "col"),
        P("segment", "col"),
        P("segment", "col", None),
        P("segment", "col", None),
    )
    out_specs = (P("segment", "col", None), P("col", None))
    return jax.shard_map(column, mesh=mesh, in_specs=in_specs, out_specs=out_specs, check_vma=False)
```

```python
import jax
import jax.numpy as jnp
from jax import lax
from jax.experimental import pallas as pl
from jax.experimental.pallas import tpu as pltpu
from jax.sharding import PartitionSpec as P

D = 8192
F = 14336
K = 4096
SEQLEN = 64
QLEN = 16
DAMP = 0.1

LAYERS = 8
W = 256
NCH = D // W
NZ = 4
NUP = NZ * (LAYERS - 1)
S_E, S_G1, S_H1, S_G2, S_H2, S_BIG, S_SMALL, N_S = range(8)
R_E1, R_E2, R_E3, R_G1, R_H1, R_H2, R_H3 = range(7)
R_G2, R_G3, R_PAIR, R_R1, R_R2, R_P1, R_P2, R_P3, N_R = range(7, 25, 2)
SLOTS = 2 * NCH
T_H1S, T_G1, T_H1, T_H2, T_H3 = 8, 10, 18, 43, 54
T_G2 = (17, 21)
T_G3 = (19, 23)
T_R1 = (38, 42)
T_R2 = (45, 49)
T_P1 = (51, 54)
T_P2 = (59, 62)
PER_P = 8
KB = 512
HALF = D // 2
STORES = 4
CHAIN = True
COL = True

f32 = jnp.float32
bf16 = jnp.bfloat16
MESH = pl.DeviceIdType.MESH


def remote(src, dst, ssem, rsem, dev):
    return pltpu.make_async_remote_copy(
        src_ref=src, dst_ref=dst, send_sem=ssem, recv_sem=rsem, device_id=dev, device_id_type=MESH
    )


def split(v):
    hi = v.astype(bf16)
    return hi, (v - hi.astype(f32)).astype(bf16)


def kernel(
    inc, hid, bas, eig, qg, qh,
    out, scores,
    own, down, rcv, ups, upr, fin, hidv, basv, bhl, eigv, qgr, qhr,
    g16, h16, a1g, a1h, qgv, qhv, ebs, ebr,
    part_out, part_in, kept, mine, r1s, r1r, r2s, r2r, prec,
    wmat, accp, gm, hm, share,
    ld_sem, out_sem, chain_s, chain_r, up_s, up_r, cs, cr, zs, zr,
):
    z = lax.axis_index("segment")
    col = lax.axis_index("col")
    c = lax.rem(col, 2)
    x = lax.rem(col // 2, 4)
    y = col // 8
    a1 = x + c * (y - x)
    a2 = y + c * (x - y)
    step1 = 2 + 6 * c
    step2 = 8 - 6 * c
    depth = LAYERS - 1 - z

    def on1(s):
        return (z, col + (lax.rem(a1 + s, 4) - a1) * step1)

    def on2(s):
        return (z, col + (lax.rem(a2 + s, 4) - a2) * step2)

    def onz(s):
        return (lax.rem(z + s, LAYERS), col)

    sibling = (z, col + 1 - 2 * c)

    barrier = pltpu.get_barrier_semaphore()
    greeted = [sibling] + [on1(s) for s in (1, 2, 3)] + [on2(s) for s in (1, 2, 3)]
    greeted += [onz(1), onz(LAYERS - 1)]
    for dev in greeted:
        pl.semaphore_signal(barrier, inc=1, device_id=dev, device_id_type=MESH)

    load_own = pltpu.make_async_copy(inc.at[0], own, ld_sem.at[0])
    load_bas = pltpu.make_async_copy(bas.at[0], basv, ld_sem.at[1])
    load_hid = pltpu.make_async_copy(hid.at[0], hidv, ld_sem.at[2])
    small = [
        pltpu.make_async_copy(eig, eigv, ld_sem.at[3]),
        pltpu.make_async_copy(qg, qgr, ld_sem.at[4]),
        pltpu.make_async_copy(qh, qhr, ld_sem.at[5]),
    ]
    for copy in small + [load_own, load_bas, load_hid]:
        copy.start()

    def fold(q, wide):
        rows = q[0].astype(f32)
        return jnp.concatenate([rows[:, s * wide:(s + 1) * wide] for s in range(4)], axis=0).astype(bf16)

    pl.semaphore_wait(barrier, len(greeted))
    for copy in small:
        copy.wait()
    g16[...] = fold(qgr, D // 4)
    h16[...] = fold(qhr, F // 4)
    ebs[0] = jnp.broadcast_to(eigv[...], (8, 128))

    def post(src, dst, dev, send, recv):
        copy = remote(src, dst, cs.at[send], cr.at[recv], dev)
        copy.start()

    def arrived(like, recv):
        remote(like, like, cs.at[0], cr.at[recv], sibling).wait_recv()

    def link(i, t):
        return remote(down.at[i], rcv.at[i], chain_s, chain_r.at[t], onz(LAYERS - 1))

    def uplink(n):
        return remote(ups.at[n], upr.at[n], up_s, up_r.at[n], onz(1))

    def lanes(i):
        return pl.ds(pl.multiple_of(i * W, W), W)

    def add(p, q):
        return (p.astype(f32) + q.astype(f32)).astype(bf16)

    def finish_chunk(i, value):
        fin[:, lanes(i)] = value
        pltpu.make_async_copy(fin.at[:, lanes(i)], out.at[0, :, lanes(i)], out_sem).start()

    def chunk_at(t):
        return lax.rem(t + NCH - NZ * depth, NCH)

    def chain_step(t):
        i = chunk_at(t)
        fed = jnp.logical_and(z < LAYERS - 1, t >= NZ)

        @pl.when(fed)
        def _():
            link(i, t - NZ).wait_recv()
            down[i] = add(own[:, lanes(i)], rcv[i])

        @pl.when(jnp.logical_not(fed))
        def _():
            down[i] = own[:, lanes(i)]

        @pl.when(jnp.logical_and(z > 0, t < NCH - NZ))
        def _():
            link(i, t).start()

        partial = t < NZ * depth

        @pl.when(jnp.logical_not(partial))
        def _():
            finish_chunk(i, down[i])

        @pl.when(jnp.logical_and(partial, t // NZ >= LAYERS // 2))
        def _():
            finish_chunk(i, add(down[i], upr[i - (NCH - NUP)]))

    def up_step(t):
        hop = t // NZ
        cut = lax.rem(z - hop + LAYERS, LAYERS)

        @pl.when(cut > 0)
        def _():
            n = (cut - 1) * NZ + t - hop * NZ
            i = NCH - NUP + n
            last = hop == LAYERS - 1

            @pl.when(hop > 0)
            def _():
                uplink(n).wait_recv()

            @pl.when(jnp.logical_and(z >= cut, hop > 0))
            def _():
                ups[n] = add(own[:, lanes(i)], upr[n])

            @pl.when(jnp.logical_and(z >= cut, hop == 0))
            def _():
                ups[n] = own[:, lanes(i)]

            @pl.when(jnp.logical_and(z < cut, jnp.logical_not(last)))
            def _():
                ups[n] = upr[n]

            @pl.when(jnp.logical_not(last))
            def _():
                uplink(n).start()

            @pl.when(jnp.logical_and(z < cut, cut - z <= LAYERS // 2))
            def _():
                finish_chunk(i, add(down[i], upr[n]))

    now = [0]

    def slots(n, fn=None):
        if CHAIN:
            ahead = min(n, SLOTS - now[0])
        else:
            ahead = 0
        base = now[0]

        def step(j, _):
            t = base + j

            @pl.when(lax.rem(t, 2) == 0)
            def _():
                chain_step(t // 2)

            @pl.when(lax.rem(t, 2) == 1)
            def _():
                up_step(t // 2)

            if fn is not None:
                fn(j)
            return 0

        if ahead:
            lax.fori_loop(0, ahead, step, 0)
        if fn is not None and n > ahead:
            lax.fori_loop(ahead, n, lambda j, _: (fn(j), 0)[1], 0)
        now[0] = min(base + n, SLOTS)

    def until(t):
        if now[0] < t:
            slots(t - now[0])

    if COL:
        for s in (1, 2, 3):
            post(ebs.at[0], ebr.at[s - 1], on1(s), S_E, R_E1)
        for s in (2, 1, 3):
            post(g16, a1g.at[pl.ds(a1 * 16, 16)], on1(s), S_G1, R_G1)

    load_own.wait()

    def order16():
        r = lax.broadcasted_iota(jnp.int32, (64, 64), 0)
        k = lax.broadcasted_iota(jnp.int32, (64, 64), 1)
        src = ((r % 16) // 4) * 16 + (r // 16) * 4 + r % 4
        return (k == src).astype(f32).astype(bf16)

    def rows16(s):
        return pl.ds(pl.multiple_of(c * 64 + lax.rem(a2 + 4 - s, 4) * 16, 16), 16)

    def assemble(a, q, wide):
        part = jnp.dot(order16(), a[...], preferred_element_type=f32).astype(bf16)
        for s in range(4):
            q[rows16(0), s * wide:(s + 1) * wide] = part[s * 16:(s + 1) * 16]

    def share_rows(q, s, dev, send, recv):
        post(q.at[rows16(s)], q.at[rows16(s)], dev, send, recv)

    def share_half(s, half, dev, recv):
        part = qgv.at[rows16(s), half * HALF:(half + 1) * HALF]
        post(part, part, dev, S_G2, recv + half)

    if COL:
        a1g[pl.ds(pl.multiple_of(a1 * 16, 16), 16)] = g16[...]
        a1h[pl.ds(pl.multiple_of(a1 * 16, 16), 16)] = h16[...]
        until(T_H1S)
        for s in (2, 1, 3):
            post(h16, a1h.at[pl.ds(a1 * 16, 16)], on1(s), S_H1, R_H1)
        until(T_G1)
        arrived(ebr.at[0:3], R_E1)
        ebs[1] = ebs[0] + ebr[0] + ebr[1] + ebr[2]
        for s in (1, 2, 3):
            post(ebs.at[1], ebr.at[2 + s], on2(s), S_E, R_E2)
        arrived(a1g.at[0:48], R_G1)
        assemble(a1g, qgv, D // 4)
        for half in (0, 1):
            for s in (2, 1, 3):
                share_half(0, half, on2(s), R_G2)
        for half in (0, 1):
            share_half(0, half, sibling, R_G3)

        load_bas.wait()

        def split_basis(j):
            for k in (0, 1):
                at = pl.ds(pl.multiple_of((2 * j + k) * KB, KB), KB)
                hi, lo = split(basv[at])
                bhl[at, 0:128] = hi
                bhl[at, 128:256] = lo

        accp[...] = jnp.zeros_like(accp)

        def project(half):
            arrived(qgv.at[0:64, 0:HALF], R_G3 + half)

            def blocks(j):
                for k in range(PER_P):
                    at = pl.ds(pl.multiple_of(half * HALF + (PER_P * j + k) * KB, KB), KB)
                    accp[...] += jnp.dot(qgv[:, at], bhl[at], preferred_element_type=f32)

            slots(HALF // KB // PER_P, blocks)

        def swap_half(half):
            arrived(qgv.at[0:48, 0:HALF], R_G2 + half)
            for s in (1, 2, 3):
                share_half(s, half, sibling, R_G3)

        slots(7, split_basis)
        until(T_G2[0])
        swap_half(0)
        until(T_H1)
        arrived(a1h.at[0:48], R_H1)
        assemble(a1h, qhv, F // 4)
        for s in (2, 1, 3):
            share_rows(qhv, 0, on2(s), S_H2, R_H2)
        share_rows(qhv, 0, sibling, S_H2, R_H3)
        split_basis(7)
        arrived(ebr.at[3:6], R_E2)
        ebs[2] = ebs[1] + ebr[3] + ebr[4] + ebr[5]
        post(ebs.at[2], ebr.at[6], sibling, S_E, R_E3)
        until(T_G3[0])
        project(0)
        until(T_G2[1])
        swap_half(1)
        until(T_G3[1])
        arrived(ebr.at[6:7], R_E3)
        ebs[3] = ebs[2] + ebr[6]
        project(1)
        damping = DAMP * jnp.sum(ebs[3][0:1], axis=1, keepdims=True) / K
        weighted = (accp[:, :128] + accp[:, 128:]) / (eigv[...] + damping)
        wmat[...] = weighted.T.astype(bf16)

        def expand(side, half):
            at = pl.ds(pl.multiple_of(side * 4096 + half * 2048, 2048), 2048)
            return jnp.dot(bhl[at, 0:128], wmat[...], preferred_element_type=f32)

        def block_rows(block, half):
            return pl.ds(pl.multiple_of(half * 2048 + block * KB, KB), KB)

        def give(half):
            at = pl.ds(half * 2048, 2048)
            part_out[at] = expand(1 - c, half).astype(bf16)
            post(part_out.at[at], part_in.at[at], sibling, S_BIG, R_PAIR + half)

        def keep(half):
            kept[pl.ds(half * 2048, 2048)] = expand(c, half)

        def add_pair(half):
            arrived(part_in.at[0:2048], R_PAIR + half)
            for s in (2, 1, 3, 0):
                at = block_rows(lax.rem(a1 + s, 4), half)
                total = kept[at] + part_in[at].astype(f32)
                if s:
                    r1s[at] = total.astype(bf16)
                    post(r1s.at[at], r1r.at[s - 1, pl.ds(half * KB, KB)], on1(s), S_BIG, R_R1 + half)
                else:
                    mine[pl.ds(half * KB, KB)] = total

        give(0)
        slots(1)
        give(1)
        keep(0)
        slots(1)
        keep(1)
        slots(1)
        add_pair(0)
        slots(1)
        add_pair(1)

        def match_hidden(j):
            for k in range(4):
                at = pl.ds(pl.multiple_of((4 * j + k) * 512, 512), 512)
                hm[...] += lax.dot_general(
                    hidv[:, at], qhv[:, at], (((1,), (1,)), ((), ())), preferred_element_type=f32
                )

        def sum_first(half):
            arrived(prec.at[0:3 * KB], R_R1 + half)
            for s in (2, 1, 3, 0):
                at = pl.ds(pl.multiple_of(half * KB + lax.rem(a2 + s, 4) * 128, 128), 128)
                total = mine[at] + r1r[0, at].astype(f32) + r1r[1, at].astype(f32) + r1r[2, at].astype(f32)
                if s:
                    r2s[at] = total.astype(bf16)
                    post(r2s.at[at], r2r.at[s - 1, pl.ds(half * 128, 128)], on2(s), S_SMALL, R_R2 + half)
                else:
                    mine[at] = total

        def sum_second(half):
            arrived(prec.at[0:384], R_R2 + half)
            at = pl.ds(pl.multiple_of(half * KB + a2 * 128, 128), 128)
            got = pl.ds(half * 128, 128)
            total = mine[at] + r2r[0, got].astype(f32) + r2r[1, got].astype(f32) + r2r[2, got].astype(f32)
            rows = pl.ds(pl.multiple_of(c * 4096 + half * 2048 + a1 * KB + a2 * 128, 128), 128)
            prec[rows] = total.astype(bf16)
            for s in (2, 1, 3):
                post(prec.at[rows], prec.at[rows], on2(s), S_SMALL, R_P1 + half)

        def band(s, half):
            return pl.ds(pl.multiple_of(c * 4096 + half * 2048 + lax.rem(a1 + 4 - s, 4) * KB, KB), KB)

        def gather_first(half):
            arrived(prec.at[0:384], R_P1 + half)
            rows = band(0, half)
            for s in (2, 1, 3):
                post(prec.at[rows], prec.at[rows], on1(s), S_BIG, R_P2 + half)
            post(prec.at[rows], prec.at[rows], sibling, S_BIG, R_P3 + half)

        def gather_second(half):
            arrived(prec.at[0:3 * KB], R_P2 + half)
            for s in (1, 2, 3):
                rows = band(s, half)
                post(prec.at[rows], prec.at[rows], sibling, S_BIG, R_P3 + half)

        until(T_R1[0])
        sum_first(0)
        until(T_R1[1])
        sum_first(1)
        until(T_H2)
        arrived(qhv.at[0:48], R_H2)
        for s in (1, 2, 3):
            share_rows(qhv, s, sibling, S_H2, R_H3)
        for half in (0, 1):
            until(T_R2[half])
            sum_second(half)
        for half in (0, 1):
            until(T_P1[half])
            gather_first(half)
        until(T_H3)
        load_hid.wait()
        arrived(qhv.at[0:64], R_H3)
        hm[...] = jnp.zeros_like(hm)
        slots(F // 2048, match_hidden)

        gm[...] = jnp.zeros_like(gm)
        GROUP = KB // W

        def match_group(first):
            features = pl.ds(pl.multiple_of(first * W, KB), KB)
            gm[...] += jnp.dot(fin[:, features], prec[features], preferred_element_type=f32)

        def first_chunk(own_side, s, half):
            side, at = (c, a1) if own_side else (1 - c, a2)
            return side * (NCH // 2) + half * (NCH // 4) + lax.rem(at + 4 - s, 4) * GROUP

        def done_at(first):
            t = lax.rem(first + NZ * depth, NCH)
            other = NZ * (LAYERS - 1 - t // NZ) + lax.rem(t, NZ)
            return 2 * (jnp.where(t < NZ * depth, jnp.maximum(t, other), t) + GROUP - 1) + 1

        late = []

        def early(own_side, half):
            seen = now[0]
            if not CHAIN or seen >= SLOTS:
                for j in range(4):
                    match_group(first_chunk(own_side, j, half))
                return

            def two(j):
                for k in (0, 1):
                    first = first_chunk(own_side, 2 * j + k, half)

                    @pl.when(done_at(first) < seen)
                    def _(first=first):
                        match_group(first)

            slots(2, two)
            late.append((own_side, half, seen))

        until(T_P2[0])
        gather_second(0)
        early(True, 0)
        until(T_P2[1])
        gather_second(1)
        arrived(prec.at[0:2048], R_P3)
        early(False, 0)
        until(SLOTS)
        early(True, 1)
        arrived(prec.at[0:2048], R_P3 + 1)
        early(False, 1)
        for own_side, half, seen in late:
            for j in range(4):
                first = first_chunk(own_side, j, half)

                @pl.when(done_at(first) >= seen)
                def _(first=first):
                    match_group(first)
    else:
        load_bas.wait()
        load_hid.wait()
        until(SLOTS)

    if COL:
        prod = gm[...] * hm[...]
        pos = lax.broadcasted_iota(jnp.int32, (128, 128), 0)
        side = pos // 64
        p2nd = (pos // 16) % 4
        p1st = (pos // 4) % 4
        query = jnp.where(side == 0, p2nd * 2 + p1st // 2, p1st * 2 + p2nd // 2)
        pick = (query == lax.broadcasted_iota(jnp.int32, (128, 128), 1)).astype(f32)
        sums = [jnp.sum(prod[s * SEQLEN:(s + 1) * SEQLEN], axis=0, keepdims=True) for s in (0, 1)]
        line = lax.broadcasted_iota(jnp.int32, (8, 128), 0)
        both = jnp.where(line == 0, sums[0], jnp.where(line == 1, sums[1], 0.0))
        tile = jnp.dot(both, pick, precision=lax.Precision.HIGHEST, preferred_element_type=f32)
        share[z] = tile / (SEQLEN * QLEN)
        for s in (4, 3, 5, 2, 6, 1, 7):
            remote(share.at[z], share.at[z], zs, zr, onz(s)).start()
        for like, kind in (
            (ebr, S_E),
            (a1g.at[0:48], S_G1),
            (a1h.at[0:48], S_H1),
            (qgv.at[0:112], S_G2),
            (qhv.at[0:112], S_H2),
            (bhl.at[0:7168], S_BIG),
            (prec.at[0:1536], S_SMALL),
        ):
            remote(like, like, cs.at[kind], cr.at[0], sibling).wait_send()
    if CHAIN:
        pltpu.make_async_copy(fin, out.at[0], out_sem).wait()

        @pl.when(z > 0)
        def _():
            sends = pl.ds(0, NCH - NZ)
            remote(down.at[sends], rcv.at[sends], chain_s, chain_r.at[0], onz(LAYERS - 1)).wait_send()

        @pl.when(z < LAYERS - 1)
        def _():
            sends = pl.ds(0, NUP - NZ)
            remote(ups.at[sends], upr.at[sends], up_s, up_r.at[0], onz(1)).wait_send()

        @pl.when(z == LAYERS - 1)
        def _():
            remote(ups, upr, up_s, up_r.at[0], onz(1)).wait_send()

    if COL:
        others = remote(share.at[0:LAYERS - 1], share.at[0:LAYERS - 1], zs, zr, sibling)
        others.wait_recv()
        total = share[0]
        for s in range(1, LAYERS):
            total = total + share[s]
        scores[...] = total[0:2, 0:8]
        others.wait_send()


def store(section, scores, section_out, scores_out, sem):
    rows = 128 // STORES
    copies = [
        pltpu.make_async_copy(section.at[0, pl.ds(k * rows, rows)], section_out.at[0, pl.ds(k * rows, rows)], sem.at[k])
        for k in range(STORES)
    ]
    copies.append(pltpu.make_async_copy(scores, scores_out, sem.at[STORES]))
    for copy in copies:
        copy.start()
    for copy in copies:
        copy.wait()


def column(incoming, hidden, basis, eigvals, query_grads, query_hidden):
    hbm = pl.BlockSpec(memory_space=pltpu.HBM)
    vmem = pl.BlockSpec(memory_space=pltpu.VMEM)
    dma = pltpu.SemaphoreType.DMA
    section, scores = pl.pallas_call(
        kernel,
        out_shape=(
            pltpu.VMEM((1, 128, D), bf16),
            pltpu.VMEM((2, 8), f32),
        ),
        in_specs=[hbm] * 6,
        out_specs=(pl.BlockSpec(memory_space=pl.ANY), vmem),
        scratch_shapes=[
            pltpu.VMEM((128, D), bf16),
            pltpu.VMEM((NCH, 128, W), bf16),
            pltpu.VMEM((NCH, 128, W), bf16),
            pltpu.VMEM((NUP, 128, W), bf16),
            pltpu.VMEM((NUP, 128, W), bf16),
            pltpu.VMEM((128, D), bf16),
            pltpu.VMEM((128, F), bf16),
            pltpu.VMEM((D, 128), f32),
            pltpu.VMEM((D, 256), bf16),
            pltpu.VMEM((1, 128), f32),
            pltpu.VMEM((1, 4, D), bf16),
            pltpu.VMEM((1, 4, F), bf16),
            pltpu.VMEM((16, D // 4), bf16),
            pltpu.VMEM((16, F // 4), bf16),
            pltpu.VMEM((64, D // 4), bf16),
            pltpu.VMEM((64, F // 4), bf16),
            pltpu.VMEM((128, D), bf16),
            pltpu.VMEM((128, F), bf16),
            pltpu.VMEM((4, 8, 128), f32),
            pltpu.VMEM((7, 8, 128), f32),
            pltpu.VMEM((4096, 128), bf16),
            pltpu.VMEM((4096, 128), bf16),
            pltpu.VMEM((4096, 128), f32),
            pltpu.VMEM((1024, 128), f32),
            pltpu.VMEM((4096, 128), bf16),
            pltpu.VMEM((3, 1024, 128), bf16),
            pltpu.VMEM((1024, 128), bf16),
            pltpu.VMEM((3, 256, 128), bf16),
            pltpu.VMEM((D, 128), bf16),
            pltpu.VMEM((128, 128), bf16),
            pltpu.VMEM((128, 256), f32),
            pltpu.VMEM((128, 128), f32),
            pltpu.VMEM((128, 128), f32),
            pltpu.VMEM((LAYERS, 8, 128), f32),
            dma((6,)),
            dma,
            dma,
            dma((NCH - NZ,)),
            dma,
            dma((NUP,)),
            dma((N_S,)),
            dma((N_R,)),
            dma,
            dma,
        ],
        compiler_params=pltpu.CompilerParams(
            collective_id=0, has_side_effects=True, vmem_limit_bytes=60 * 1024 * 1024
        ),
    )(incoming, hidden, basis, eigvals, query_grads, query_hidden)
    anyspace = pl.BlockSpec(memory_space=pl.ANY)
    return pl.pallas_call(
        store,
        out_shape=(
            jax.ShapeDtypeStruct((1, 128, D), bf16),
            jax.ShapeDtypeStruct((2, 8), f32),
        ),
        in_specs=[anyspace, anyspace],
        out_specs=(hbm, hbm),
        scratch_shapes=[dma((STORES + 1,))],
        compiler_params=pltpu.CompilerParams(vmem_limit_bytes=1024 * 1024),
    )(section, scores)


def solution(mesh):
    in_specs = (
        P("segment", "col", None),
        P("segment", "col", None),
        P("segment", None, "col"),
        P("segment", "col"),
        P("segment", "col", None),
        P("segment", "col", None),
    )
    out_specs = (P("segment", "col", None), P("col", None))
    return jax.shard_map(column, mesh=mesh, in_specs=in_specs, out_specs=out_specs, check_vma=False)
```

```python
import jax
import jax.numpy as jnp
from jax import lax
from jax.experimental import pallas as pl
from jax.experimental.pallas import tpu as pltpu
from jax.sharding import PartitionSpec as P

D = 8192
F = 14336
K = 4096
SEQLEN = 64
QLEN = 16
DAMP = 0.1

LAYERS = 8
W = 256
NCH = D // W
NZ = 4
NUP = NZ * (LAYERS - 1)
S_E, S_G1, S_H1, S_G2, S_H2, S_BIG, S_SMALL, N_S = range(8)
R_E1, R_E2, R_E3, R_G1, R_H1, R_H2, R_H3 = range(7)
R_G2, R_G3, R_PAIR, R_R1, R_R2, R_P1, R_P2, R_P3, N_R = range(7, 25, 2)
SLOTS = 2 * NCH
T_H1S, T_G1, T_H1, T_H2, T_H3 = 8, 8, 18, 43, 54
T_G2 = (17, 21)
T_G3 = (19, 23)
T_R1 = (38, 42)
T_R2 = (45, 49)
T_P1 = (51, 54)
T_P2 = (57, 60)
PER_P = 8
KB = 512
HALF = D // 2
AHEAD = 14
STORES = 4
CHAIN = True
COL = True

f32 = jnp.float32
bf16 = jnp.bfloat16
MESH = pl.DeviceIdType.MESH


def remote(src, dst, ssem, rsem, dev):
    return pltpu.make_async_remote_copy(
        src_ref=src, dst_ref=dst, send_sem=ssem, recv_sem=rsem, device_id=dev, device_id_type=MESH
    )


def split(v):
    hi = v.astype(bf16)
    return hi, (v - hi.astype(f32)).astype(bf16)


def kernel(
    inc, hid, bas, eig, qg, qh,
    out, scores,
    own, down, rcv, ups, upr, fin, hidv, basv, bhl, eigv, qgr, qhr,
    g16, h16, a1g, a1h, qgv, qhv, ebs, ebr,
    part_out, part_in, kept, mine, r1s, r1r, r2s, r2r, prec,
    wmat, accp, gm, hm, share,
    ld_sem, out_sem, chain_s, chain_r, up_s, up_r, cs, cr, zs, zr,
):
    z = lax.axis_index("segment")
    col = lax.axis_index("col")
    c = lax.rem(col, 2)
    x = lax.rem(col // 2, 4)
    y = col // 8
    a1 = x + c * (y - x)
    a2 = y + c * (x - y)
    step1 = 2 + 6 * c
    step2 = 8 - 6 * c
    depth = LAYERS - 1 - z

    def on1(s):
        return (z, col + (lax.rem(a1 + s, 4) - a1) * step1)

    def on2(s):
        return (z, col + (lax.rem(a2 + s, 4) - a2) * step2)

    def onz(s):
        return (lax.rem(z + s, LAYERS), col)

    sibling = (z, col + 1 - 2 * c)

    barrier = pltpu.get_barrier_semaphore()
    greeted = [sibling] + [on1(s) for s in (1, 2, 3)] + [on2(s) for s in (1, 2, 3)]
    greeted += [onz(1), onz(LAYERS - 1)]
    for dev in greeted:
        pl.semaphore_signal(barrier, inc=1, device_id=dev, device_id_type=MESH)

    load_own = pltpu.make_async_copy(inc.at[0], own, ld_sem.at[0])
    load_bas = pltpu.make_async_copy(bas.at[0], basv, ld_sem.at[1])
    load_hid = pltpu.make_async_copy(hid.at[0], hidv, ld_sem.at[2])
    small = [
        pltpu.make_async_copy(eig, eigv, ld_sem.at[3]),
        pltpu.make_async_copy(qg, qgr, ld_sem.at[4]),
        pltpu.make_async_copy(qh, qhr, ld_sem.at[5]),
    ]
    for copy in small + [load_own, load_bas, load_hid]:
        copy.start()

    def fold(q, wide):
        rows = q[0].astype(f32)
        return jnp.concatenate([rows[:, s * wide:(s + 1) * wide] for s in range(4)], axis=0).astype(bf16)

    pl.semaphore_wait(barrier, len(greeted))
    for copy in small:
        copy.wait()
    g16[...] = fold(qgr, D // 4)
    h16[...] = fold(qhr, F // 4)
    ebs[0] = jnp.broadcast_to(eigv[...], (8, 128))

    def post(src, dst, dev, send, recv):
        copy = remote(src, dst, cs.at[send], cr.at[recv], dev)
        copy.start()

    def arrived(like, recv):
        remote(like, like, cs.at[0], cr.at[recv], sibling).wait_recv()

    def link(i, t):
        return remote(down.at[i], rcv.at[i], chain_s, chain_r.at[lax.rem(t, AHEAD)], onz(LAYERS - 1))

    def uplink(n):
        return remote(ups.at[n], upr.at[n], up_s, up_r.at[n], onz(1))

    def lanes(i):
        return pl.ds(pl.multiple_of(i * W, W), W)

    def add(p, q):
        return (p.astype(f32) + q.astype(f32)).astype(bf16)

    def finish_chunk(i, value):
        fin[:, lanes(i)] = value
        pltpu.make_async_copy(fin.at[:, lanes(i)], out.at[0, :, lanes(i)], out_sem).start()

    def chunk_at(t):
        return lax.rem(t + NCH - NZ * depth, NCH)

    def chain_step(t):
        i = chunk_at(t)
        fed = jnp.logical_and(z < LAYERS - 1, t >= NZ)

        @pl.when(fed)
        def _():
            link(i, t - NZ).wait_recv()
            down[i] = add(own[:, lanes(i)], rcv[i])

        @pl.when(jnp.logical_not(fed))
        def _():
            down[i] = own[:, lanes(i)]

        @pl.when(jnp.logical_and(z > 0, t < NCH - NZ))
        def _():
            link(i, t).start()

        partial = t < NZ * depth

        @pl.when(jnp.logical_not(partial))
        def _():
            finish_chunk(i, down[i])

        @pl.when(jnp.logical_and(partial, t // NZ >= LAYERS // 2))
        def _():
            finish_chunk(i, add(down[i], upr[i - (NCH - NUP)]))

    def up_step(t):
        hop = t // NZ
        cut = lax.rem(z - hop + LAYERS, LAYERS)

        @pl.when(cut > 0)
        def _():
            n = (cut - 1) * NZ + t - hop * NZ
            i = NCH - NUP + n
            last = hop == LAYERS - 1

            @pl.when(hop > 0)
            def _():
                uplink(n).wait_recv()

            @pl.when(jnp.logical_and(z >= cut, hop > 0))
            def _():
                ups[n] = add(own[:, lanes(i)], upr[n])

            @pl.when(jnp.logical_and(z >= cut, hop == 0))
            def _():
                ups[n] = own[:, lanes(i)]

            @pl.when(jnp.logical_and(z < cut, jnp.logical_not(last)))
            def _():
                ups[n] = upr[n]

            @pl.when(jnp.logical_not(last))
            def _():
                uplink(n).start()

            @pl.when(jnp.logical_and(z < cut, cut - z <= LAYERS // 2))
            def _():
                finish_chunk(i, add(down[i], upr[n]))

    now = [0]

    def slots(n, fn=None):
        if CHAIN:
            ahead = min(n, SLOTS - now[0])
        else:
            ahead = 0
        base = now[0]

        def step(j, _):
            t = base + j

            @pl.when(lax.rem(t, 2) == 0)
            def _():
                chain_step(t // 2)

            @pl.when(lax.rem(t, 2) == 1)
            def _():
                up_step(t // 2)

            if fn is not None:
                fn(j)
            return 0

        if ahead:
            lax.fori_loop(0, ahead, step, 0)
        if fn is not None and n > ahead:
            lax.fori_loop(ahead, n, lambda j, _: (fn(j), 0)[1], 0)
        now[0] = min(base + n, SLOTS)

    def until(t):
        if now[0] < t:
            slots(t - now[0])

    if COL:
        for s in (1, 2, 3):
            post(ebs.at[0], ebr.at[s - 1], on1(s), S_E, R_E1)
        for s in (2, 1, 3):
            post(g16, a1g.at[pl.ds(a1 * 16, 16)], on1(s), S_G1, R_G1)

    load_own.wait()

    def order16():
        r = lax.broadcasted_iota(jnp.int32, (64, 64), 0)
        k = lax.broadcasted_iota(jnp.int32, (64, 64), 1)
        src = ((r % 16) // 4) * 16 + (r // 16) * 4 + r % 4
        return (k == src).astype(f32).astype(bf16)

    def rows16(s):
        return pl.ds(pl.multiple_of(c * 64 + lax.rem(a2 + 4 - s, 4) * 16, 16), 16)

    def assemble(a, q, wide):
        part = jnp.dot(order16(), a[...], preferred_element_type=f32).astype(bf16)
        for s in range(4):
            q[rows16(0), s * wide:(s + 1) * wide] = part[s * 16:(s + 1) * 16]

    def share_rows(q, s, dev, send, recv):
        post(q.at[rows16(s)], q.at[rows16(s)], dev, send, recv)

    def share_half(s, half, dev, recv):
        part = qgv.at[rows16(s), half * HALF:(half + 1) * HALF]
        post(part, part, dev, S_G2, recv + half)

    if COL:
        a1g[pl.ds(pl.multiple_of(a1 * 16, 16), 16)] = g16[...]
        a1h[pl.ds(pl.multiple_of(a1 * 16, 16), 16)] = h16[...]
        until(T_H1S)
        for s in (2, 1, 3):
            post(h16, a1h.at[pl.ds(a1 * 16, 16)], on1(s), S_H1, R_H1)
        until(T_G1)
        arrived(ebr.at[0:3], R_E1)
        ebs[1] = ebs[0] + ebr[0] + ebr[1] + ebr[2]
        for s in (1, 2, 3):
            post(ebs.at[1], ebr.at[2 + s], on2(s), S_E, R_E2)
        arrived(a1g.at[0:48], R_G1)
        assemble(a1g, qgv, D // 4)
        for half in (0, 1):
            for s in (2, 1, 3):
                share_half(0, half, on2(s), R_G2)
        for half in (0, 1):
            share_half(0, half, sibling, R_G3)

        load_bas.wait()

        def split_basis(j):
            for k in (0, 1):
                at = pl.ds(pl.multiple_of((2 * j + k) * KB, KB), KB)
                hi, lo = split(basv[at])
                bhl[at, 0:128] = hi
                bhl[at, 128:256] = lo

        accp[...] = jnp.zeros_like(accp)

        def project(half):
            arrived(qgv.at[0:64, 0:HALF], R_G3 + half)

            def blocks(j):
                for k in range(PER_P):
                    at = pl.ds(pl.multiple_of(half * HALF + (PER_P * j + k) * KB, KB), KB)
                    accp[...] += jnp.dot(qgv[:, at], bhl[at], preferred_element_type=f32)

            slots(HALF // KB // PER_P, blocks)

        def swap_half(half):
            arrived(qgv.at[0:48, 0:HALF], R_G2 + half)
            for s in (1, 2, 3):
                share_half(s, half, sibling, R_G3)

        slots(7, split_basis)
        until(T_G2[0])
        swap_half(0)
        until(T_H1)
        arrived(a1h.at[0:48], R_H1)
        assemble(a1h, qhv, F // 4)
        for s in (2, 1, 3):
            share_rows(qhv, 0, on2(s), S_H2, R_H2)
        share_rows(qhv, 0, sibling, S_H2, R_H3)
        split_basis(7)
        arrived(ebr.at[3:6], R_E2)
        ebs[2] = ebs[1] + ebr[3] + ebr[4] + ebr[5]
        post(ebs.at[2], ebr.at[6], sibling, S_E, R_E3)
        until(T_G3[0])
        project(0)
        until(T_G2[1])
        swap_half(1)
        until(T_G3[1])
        arrived(ebr.at[6:7], R_E3)
        ebs[3] = ebs[2] + ebr[6]
        project(1)
        damping = DAMP * jnp.sum(ebs[3][0:1], axis=1, keepdims=True) / K
        weighted = (accp[:, :128] + accp[:, 128:]) / (eigv[...] + damping)
        wmat[...] = weighted.T.astype(bf16)

        def expand(side, half):
            at = pl.ds(pl.multiple_of(side * 4096 + half * 2048, 2048), 2048)
            return jnp.dot(bhl[at, 0:128], wmat[...], preferred_element_type=f32)

        def block_rows(block, half):
            return pl.ds(pl.multiple_of(half * 2048 + block * KB, KB), KB)

        def give(half):
            at = pl.ds(half * 2048, 2048)
            part_out[at] = expand(1 - c, half).astype(bf16)
            post(part_out.at[at], part_in.at[at], sibling, S_BIG, R_PAIR + half)

        def keep(half):
            kept[pl.ds(half * 2048, 2048)] = expand(c, half)

        def add_pair(half):
            arrived(part_in.at[0:2048], R_PAIR + half)
            for s in (2, 1, 3, 0):
                at = block_rows(lax.rem(a1 + s, 4), half)
                total = kept[at] + part_in[at].astype(f32)
                if s:
                    r1s[at] = total.astype(bf16)
                    post(r1s.at[at], r1r.at[s - 1, pl.ds(half * KB, KB)], on1(s), S_BIG, R_R1 + half)
                else:
                    mine[pl.ds(half * KB, KB)] = total

        give(0)
        slots(1)
        give(1)
        keep(0)
        slots(1)
        keep(1)
        slots(1)
        add_pair(0)
        slots(1)
        add_pair(1)

        def match_hidden(j):
            for k in range(4):
                at = pl.ds(pl.multiple_of((4 * j + k) * 512, 512), 512)
                hm[...] += lax.dot_general(
                    hidv[:, at], qhv[:, at], (((1,), (1,)), ((), ())), preferred_element_type=f32
                )

        def sum_first(half):
            arrived(prec.at[0:3 * KB], R_R1 + half)
            for s in (2, 1, 3, 0):
                at = pl.ds(pl.multiple_of(half * KB + lax.rem(a2 + s, 4) * 128, 128), 128)
                total = mine[at] + r1r[0, at].astype(f32) + r1r[1, at].astype(f32) + r1r[2, at].astype(f32)
                if s:
                    r2s[at] = total.astype(bf16)
                    post(r2s.at[at], r2r.at[s - 1, pl.ds(half * 128, 128)], on2(s), S_SMALL, R_R2 + half)
                else:
                    mine[at] = total

        def sum_second(half):
            arrived(prec.at[0:384], R_R2 + half)
            at = pl.ds(pl.multiple_of(half * KB + a2 * 128, 128), 128)
            got = pl.ds(half * 128, 128)
            total = mine[at] + r2r[0, got].astype(f32) + r2r[1, got].astype(f32) + r2r[2, got].astype(f32)
            rows = pl.ds(pl.multiple_of(c * 4096 + half * 2048 + a1 * KB + a2 * 128, 128), 128)
            prec[rows] = total.astype(bf16)
            for s in (2, 1, 3):
                post(prec.at[rows], prec.at[rows], on2(s), S_SMALL, R_P1 + half)

        def band(s, half):
            return pl.ds(pl.multiple_of(c * 4096 + half * 2048 + lax.rem(a1 + 4 - s, 4) * KB, KB), KB)

        def gather_first(half):
            arrived(prec.at[0:384], R_P1 + half)
            rows = band(0, half)
            for s in (2, 1, 3):
                post(prec.at[rows], prec.at[rows], on1(s), S_BIG, R_P2 + half)
            post(prec.at[rows], prec.at[rows], sibling, S_BIG, R_P3 + half)

        def gather_second(half):
            arrived(prec.at[0:3 * KB], R_P2 + half)
            for s in (1, 2, 3):
                rows = band(s, half)
                post(prec.at[rows], prec.at[rows], sibling, S_BIG, R_P3 + half)

        until(T_R1[0])
        sum_first(0)
        until(T_R1[1])
        sum_first(1)
        until(T_H2)
        arrived(qhv.at[0:48], R_H2)
        for s in (1, 2, 3):
            share_rows(qhv, s, sibling, S_H2, R_H3)
        for half in (0, 1):
            until(T_R2[half])
            sum_second(half)
        for half in (0, 1):
            until(T_P1[half])
            gather_first(half)
        until(T_H3)
        load_hid.wait()
        arrived(qhv.at[0:64], R_H3)
        hm[...] = jnp.zeros_like(hm)
        slots(F // 2048, match_hidden)

        gm[...] = jnp.zeros_like(gm)
        GROUP = KB // W

        def match_group(first):
            features = pl.ds(pl.multiple_of(first * W, KB), KB)
            gm[...] += jnp.dot(fin[:, features], prec[features], preferred_element_type=f32)

        def first_chunk(own_side, s, half):
            side, at = (c, a1) if own_side else (1 - c, a2)
            return side * (NCH // 2) + half * (NCH // 4) + lax.rem(at + 4 - s, 4) * GROUP

        def done_at(first):
            t = lax.rem(first + NZ * depth, NCH)
            other = NZ * (LAYERS - 1 - t // NZ) + lax.rem(t, NZ)
            return 2 * (jnp.where(t < NZ * depth, jnp.maximum(t, other), t) + GROUP - 1) + 1

        late = []

        def early(own_side, half):
            seen = now[0]
            if not CHAIN or seen >= SLOTS:
                for j in range(4):
                    match_group(first_chunk(own_side, j, half))
                return

            def two(j):
                for k in (0, 1):
                    first = first_chunk(own_side, 2 * j + k, half)

                    @pl.when(done_at(first) < seen)
                    def _(first=first):
                        match_group(first)

            slots(2, two)
            late.append((own_side, half, seen))

        until(T_P2[0])
        gather_second(0)
        early(True, 0)
        until(T_P2[1])
        gather_second(1)
        arrived(prec.at[0:2048], R_P3)
        early(False, 0)
        until(SLOTS)
        early(True, 1)
        for own_side, half, seen in late:
            for j in range(4):
                first = first_chunk(own_side, j, half)

                @pl.when(done_at(first) >= seen)
                def _(first=first):
                    match_group(first)

        arrived(prec.at[0:2048], R_P3 + 1)
        early(False, 1)
    else:
        load_bas.wait()
        load_hid.wait()
        until(SLOTS)

    if COL:
        prod = gm[...] * hm[...]
        pos = lax.broadcasted_iota(jnp.int32, (128, 128), 0)
        side = pos // 64
        p2nd = (pos // 16) % 4
        p1st = (pos // 4) % 4
        query = jnp.where(side == 0, p2nd * 2 + p1st // 2, p1st * 2 + p2nd // 2)
        pick = (query == lax.broadcasted_iota(jnp.int32, (128, 128), 1)).astype(f32)
        sums = [jnp.sum(prod[s * SEQLEN:(s + 1) * SEQLEN], axis=0, keepdims=True) for s in (0, 1)]
        line = lax.broadcasted_iota(jnp.int32, (8, 128), 0)
        both = jnp.where(line == 0, sums[0], jnp.where(line == 1, sums[1], 0.0))
        tile = jnp.dot(both, pick, precision=lax.Precision.HIGHEST, preferred_element_type=f32)
        share[z] = tile / (SEQLEN * QLEN)
        for s in (4, 3, 5, 2, 6, 1, 7):
            remote(share.at[z], share.at[z], zs, zr, onz(s)).start()
        for like, kind in (
            (ebr, S_E),
            (a1g.at[0:48], S_G1),
            (a1h.at[0:48], S_H1),
            (qgv.at[0:112], S_G2),
            (qhv.at[0:112], S_H2),
            (bhl.at[0:7168], S_BIG),
            (prec.at[0:1536], S_SMALL),
        ):
            remote(like, like, cs.at[kind], cr.at[0], sibling).wait_send()
    if CHAIN:
        pltpu.make_async_copy(fin, out.at[0], out_sem).wait()

        @pl.when(z > 0)
        def _():
            sends = pl.ds(0, NCH - NZ)
            remote(down.at[sends], rcv.at[sends], chain_s, chain_r.at[0], onz(LAYERS - 1)).wait_send()

        @pl.when(z < LAYERS - 1)
        def _():
            sends = pl.ds(0, NUP - NZ)
            remote(ups.at[sends], upr.at[sends], up_s, up_r.at[0], onz(1)).wait_send()

        @pl.when(z == LAYERS - 1)
        def _():
            remote(ups, upr, up_s, up_r.at[0], onz(1)).wait_send()

    if COL:
        others = remote(share.at[0:LAYERS - 1], share.at[0:LAYERS - 1], zs, zr, sibling)
        others.wait_recv()
        total = share[0]
        for s in range(1, LAYERS):
            total = total + share[s]
        scores[...] = total[0:2, 0:8]
        others.wait_send()


def store(section, scores, section_out, scores_out, sem):
    rows = 128 // STORES
    copies = [
        pltpu.make_async_copy(section.at[0, pl.ds(k * rows, rows)], section_out.at[0, pl.ds(k * rows, rows)], sem.at[k])
        for k in range(STORES)
    ]
    copies.append(pltpu.make_async_copy(scores, scores_out, sem.at[STORES]))
    for copy in copies:
        copy.start()
    for copy in copies:
        copy.wait()


def column(incoming, hidden, basis, eigvals, query_grads, query_hidden):
    hbm = pl.BlockSpec(memory_space=pltpu.HBM)
    vmem = pl.BlockSpec(memory_space=pltpu.VMEM)
    dma = pltpu.SemaphoreType.DMA
    section, scores = pl.pallas_call(
        kernel,
        out_shape=(
            pltpu.VMEM((1, 128, D), bf16),
            pltpu.VMEM((2, 8), f32),
        ),
        in_specs=[hbm] * 6,
        out_specs=(pl.BlockSpec(memory_space=pl.ANY), vmem),
        scratch_shapes=[
            pltpu.VMEM((128, D), bf16),
            pltpu.VMEM((NCH, 128, W), bf16),
            pltpu.VMEM((NCH, 128, W), bf16),
            pltpu.VMEM((NUP, 128, W), bf16),
            pltpu.VMEM((NUP, 128, W), bf16),
            pltpu.VMEM((128, D), bf16),
            pltpu.VMEM((128, F), bf16),
            pltpu.VMEM((D, 128), f32),
            pltpu.VMEM((D, 256), bf16),
            pltpu.VMEM((1, 128), f32),
            pltpu.VMEM((1, 4, D), bf16),
            pltpu.VMEM((1, 4, F), bf16),
            pltpu.VMEM((16, D // 4), bf16),
            pltpu.VMEM((16, F // 4), bf16),
            pltpu.VMEM((64, D // 4), bf16),
            pltpu.VMEM((64, F // 4), bf16),
            pltpu.VMEM((128, D), bf16),
            pltpu.VMEM((128, F), bf16),
            pltpu.VMEM((4, 8, 128), f32),
            pltpu.VMEM((7, 8, 128), f32),
            pltpu.VMEM((4096, 128), bf16),
            pltpu.VMEM((4096, 128), bf16),
            pltpu.VMEM((4096, 128), f32),
            pltpu.VMEM((1024, 128), f32),
            pltpu.VMEM((4096, 128), bf16),
            pltpu.VMEM((3, 1024, 128), bf16),
            pltpu.VMEM((1024, 128), bf16),
            pltpu.VMEM((3, 256, 128), bf16),
            pltpu.VMEM((D, 128), bf16),
            pltpu.VMEM((128, 128), bf16),
            pltpu.VMEM((128, 256), f32),
            pltpu.VMEM((128, 128), f32),
            pltpu.VMEM((128, 128), f32),
            pltpu.VMEM((LAYERS, 8, 128), f32),
            dma((6,)),
            dma,
            dma,
            dma((AHEAD,)),
            dma,
            dma((NUP,)),
            dma((N_S,)),
            dma((N_R,)),
            dma,
            dma,
        ],
        compiler_params=pltpu.CompilerParams(
            collective_id=0, has_side_effects=True, vmem_limit_bytes=60 * 1024 * 1024
        ),
    )(incoming, hidden, basis, eigvals, query_grads, query_hidden)
    anyspace = pl.BlockSpec(memory_space=pl.ANY)
    return pl.pallas_call(
        store,
        out_shape=(
            jax.ShapeDtypeStruct((1, 128, D), bf16),
            jax.ShapeDtypeStruct((2, 8), f32),
        ),
        in_specs=[anyspace, anyspace],
        out_specs=(hbm, hbm),
        scratch_shapes=[dma((STORES + 1,))],
        compiler_params=pltpu.CompilerParams(vmem_limit_bytes=1024 * 1024),
    )(section, scores)


def solution(mesh):
    in_specs = (
        P("segment", "col", None),
        P("segment", "col", None),
        P("segment", None, "col"),
        P("segment", "col"),
        P("segment", "col", None),
        P("segment", "col", None),
    )
    out_specs = (P("segment", "col", None), P("col", None))
    return jax.shard_map(column, mesh=mesh, in_specs=in_specs, out_specs=out_specs, check_vma=False)
```

```python
import jax
import jax.numpy as jnp
from jax import lax
from jax.experimental import pallas as pl
from jax.experimental.pallas import tpu as pltpu
from jax.sharding import PartitionSpec as P

D = 8192
F = 14336
K = 4096
SEQLEN = 64
QLEN = 16
DAMP = 0.1

LAYERS = 8
W = 256
NCH = D // W
NZ = 4
NUP = NZ * (LAYERS - 1)
S_E, S_G1, S_H1, S_G2, S_H2, S_BIG, S_SMALL, N_S = range(8)
R_E1, R_E2, R_E3, R_G1, R_H1, R_H2, R_H3 = range(7)
R_G2, R_G3, R_PAIR, R_R1, R_R2, R_P1, R_P3, R_P2 = range(7, 23, 2)
N_R = R_P2 + 6
SLOTS = 2 * NCH
T_H1S, T_G1, T_H1, T_H2, T_H3 = 8, 8, 16, 43, 53
T_G2 = (17, 21)
T_G3 = (19, 23)
T_R1 = (38, 42)
T_R2 = (45, 49)
T_P1 = (51, 54)
T_P2 = (57, 60)
PER_P = 8
KB = 512
HALF = D // 2
AHEAD = 14
STORES = 1
CHAIN = True
COL = True

f32 = jnp.float32
bf16 = jnp.bfloat16
MESH = pl.DeviceIdType.MESH


def remote(src, dst, ssem, rsem, dev):
    return pltpu.make_async_remote_copy(
        src_ref=src, dst_ref=dst, send_sem=ssem, recv_sem=rsem, device_id=dev, device_id_type=MESH
    )


def split(v):
    hi = v.astype(bf16)
    return hi, (v - hi.astype(f32)).astype(bf16)


def kernel(
    inc, hid, bas, eig, qg, qh,
    out, scores,
    own, down, rcv, ups, upr, fin, hidv, basv, bhl, eigv, qgr, qhr,
    g16, h16, a1g, a1h, qgv, qhv, ebs, ebr,
    part_out, part_in, kept, mine, r1s, r1r, r2s, r2r, prec,
    wmat, accp, gm, hm, pick, share,
    ld_sem, out_sem, chain_s, chain_r, up_s, up_r, cs, cr, zs, zr,
):
    z = lax.axis_index("segment")
    col = lax.axis_index("col")
    c = lax.rem(col, 2)
    x = lax.rem(col // 2, 4)
    y = col // 8
    a1 = x + c * (y - x)
    a2 = y + c * (x - y)
    step1 = 2 + 6 * c
    step2 = 8 - 6 * c
    depth = LAYERS - 1 - z

    def on1(s):
        return (z, col + (lax.rem(a1 + s, 4) - a1) * step1)

    def on2(s):
        return (z, col + (lax.rem(a2 + s, 4) - a2) * step2)

    def onz(s):
        return (lax.rem(z + s, LAYERS), col)

    sibling = (z, col + 1 - 2 * c)

    barrier = pltpu.get_barrier_semaphore()
    greeted = [sibling] + [on1(s) for s in (1, 2, 3)] + [on2(s) for s in (1, 2, 3)]
    greeted += [onz(1), onz(LAYERS - 1)]
    for dev in greeted:
        pl.semaphore_signal(barrier, inc=1, device_id=dev, device_id_type=MESH)

    load_own = pltpu.make_async_copy(inc.at[0], own, ld_sem.at[0])
    load_bas = pltpu.make_async_copy(bas.at[0], basv, ld_sem.at[1])
    load_hid = pltpu.make_async_copy(hid.at[0], hidv, ld_sem.at[2])
    small = [
        pltpu.make_async_copy(eig, eigv, ld_sem.at[3]),
        pltpu.make_async_copy(qg, qgr, ld_sem.at[4]),
        pltpu.make_async_copy(qh, qhr, ld_sem.at[5]),
    ]
    for copy in small + [load_own, load_bas, load_hid]:
        copy.start()

    def fold(q, wide):
        rows = q[0].astype(f32)
        return jnp.concatenate([rows[:, s * wide:(s + 1) * wide] for s in range(4)], axis=0).astype(bf16)

    pl.semaphore_wait(barrier, len(greeted))
    for copy in small:
        copy.wait()
    g16[...] = fold(qgr, D // 4)
    h16[...] = fold(qhr, F // 4)
    ebs[0] = jnp.broadcast_to(eigv[...], (8, 128))

    def post(src, dst, dev, send, recv):
        copy = remote(src, dst, cs.at[send], cr.at[recv], dev)
        copy.start()

    def arrived(like, recv):
        remote(like, like, cs.at[0], cr.at[recv], sibling).wait_recv()

    def link(i, t):
        return remote(down.at[i], rcv.at[i], chain_s, chain_r.at[lax.rem(t, AHEAD)], onz(LAYERS - 1))

    def uplink(n):
        return remote(ups.at[n], upr.at[n], up_s, up_r.at[n], onz(1))

    def lanes(i):
        return pl.ds(pl.multiple_of(i * W, W), W)

    def add(p, q):
        return (p.astype(f32) + q.astype(f32)).astype(bf16)

    def finish_chunk(i, value):
        fin[:, lanes(i)] = value
        pltpu.make_async_copy(fin.at[:, lanes(i)], out.at[0, :, lanes(i)], out_sem).start()

    def chunk_at(t):
        return lax.rem(t + NCH - NZ * depth, NCH)

    def chain_step(t):
        i = chunk_at(t)
        fed = jnp.logical_and(z < LAYERS - 1, t >= NZ)

        @pl.when(fed)
        def _():
            link(i, t - NZ).wait_recv()
            down[i] = add(own[:, lanes(i)], rcv[i])

        @pl.when(jnp.logical_not(fed))
        def _():
            down[i] = own[:, lanes(i)]

        @pl.when(jnp.logical_and(z > 0, t < NCH - NZ))
        def _():
            link(i, t).start()

        partial = t < NZ * depth

        @pl.when(jnp.logical_not(partial))
        def _():
            finish_chunk(i, down[i])

        @pl.when(jnp.logical_and(partial, t // NZ >= LAYERS // 2))
        def _():
            finish_chunk(i, add(down[i], upr[i - (NCH - NUP)]))

    def up_step(t):
        hop = t // NZ
        cut = lax.rem(z - hop + LAYERS, LAYERS)

        @pl.when(cut > 0)
        def _():
            n = (cut - 1) * NZ + t - hop * NZ
            i = NCH - NUP + n
            last = hop == LAYERS - 1

            @pl.when(hop > 0)
            def _():
                uplink(n).wait_recv()

            @pl.when(jnp.logical_and(z >= cut, hop > 0))
            def _():
                ups[n] = add(own[:, lanes(i)], upr[n])

            @pl.when(jnp.logical_and(z >= cut, hop == 0))
            def _():
                ups[n] = own[:, lanes(i)]

            @pl.when(jnp.logical_and(z < cut, jnp.logical_not(last)))
            def _():
                ups[n] = upr[n]

            @pl.when(jnp.logical_not(last))
            def _():
                uplink(n).start()

            @pl.when(jnp.logical_and(z < cut, cut - z <= LAYERS // 2))
            def _():
                finish_chunk(i, add(down[i], upr[n]))

    now = [0]

    def slots(n, fn=None):
        if CHAIN:
            ahead = min(n, SLOTS - now[0])
        else:
            ahead = 0
        base = now[0]

        def step(j, _):
            t = base + j

            @pl.when(lax.rem(t, 2) == 0)
            def _():
                chain_step(t // 2)

            @pl.when(lax.rem(t, 2) == 1)
            def _():
                up_step(t // 2)

            if fn is not None:
                fn(j)
            return 0

        if ahead:
            lax.fori_loop(0, ahead, step, 0)
        if fn is not None and n > ahead:
            lax.fori_loop(ahead, n, lambda j, _: (fn(j), 0)[1], 0)
        now[0] = min(base + n, SLOTS)

    def until(t):
        if now[0] < t:
            slots(t - now[0])

    if COL:
        for s in (1, 2, 3):
            post(ebs.at[0], ebr.at[s - 1], on1(s), S_E, R_E1)
        for s in (2, 1, 3):
            post(g16, a1g.at[pl.ds(a1 * 16, 16)], on1(s), S_G1, R_G1)

    load_own.wait()

    def order16():
        r = lax.broadcasted_iota(jnp.int32, (64, 64), 0)
        k = lax.broadcasted_iota(jnp.int32, (64, 64), 1)
        src = ((r % 16) // 4) * 16 + (r // 16) * 4 + r % 4
        return (k == src).astype(f32).astype(bf16)

    def rows16(s):
        return pl.ds(pl.multiple_of(c * 64 + lax.rem(a2 + 4 - s, 4) * 16, 16), 16)

    def assemble(a, q, wide):
        part = jnp.dot(order16(), a[...], preferred_element_type=f32).astype(bf16)
        for s in range(4):
            q[rows16(0), s * wide:(s + 1) * wide] = part[s * 16:(s + 1) * 16]

    def share_rows(q, s, dev, send, recv):
        post(q.at[rows16(s)], q.at[rows16(s)], dev, send, recv)

    def share_half(s, half, dev, recv):
        part = qgv.at[rows16(s), half * HALF:(half + 1) * HALF]
        post(part, part, dev, S_G2, recv + half)

    if COL:
        a1g[pl.ds(pl.multiple_of(a1 * 16, 16), 16)] = g16[...]
        a1h[pl.ds(pl.multiple_of(a1 * 16, 16), 16)] = h16[...]
        until(T_H1S)
        for s in (2, 1, 3):
            post(h16, a1h.at[pl.ds(a1 * 16, 16)], on1(s), S_H1, R_H1)
        until(T_G1)
        arrived(ebr.at[0:3], R_E1)
        ebs[1] = ebs[0] + ebr[0] + ebr[1] + ebr[2]
        for s in (1, 2, 3):
            post(ebs.at[1], ebr.at[2 + s], on2(s), S_E, R_E2)
        arrived(a1g.at[0:48], R_G1)
        assemble(a1g, qgv, D // 4)
        for half in (0, 1):
            for s in (2, 1, 3):
                share_half(0, half, on2(s), R_G2)
        for half in (0, 1):
            share_half(0, half, sibling, R_G3)

        load_bas.wait()

        def split_basis(j):
            for k in (0, 1):
                at = pl.ds(pl.multiple_of((2 * j + k) * KB, KB), KB)
                hi, lo = split(basv[at])
                bhl[at, 0:128] = hi
                bhl[at, 128:256] = lo

        accp[...] = jnp.zeros_like(accp)

        def project(half):
            arrived(qgv.at[0:64, 0:HALF], R_G3 + half)

            def blocks(j):
                for k in range(PER_P):
                    at = pl.ds(pl.multiple_of(half * HALF + (PER_P * j + k) * KB, KB), KB)
                    accp[...] += jnp.dot(qgv[:, at], bhl[at], preferred_element_type=f32)

            slots(HALF // KB // PER_P, blocks)

        def swap_half(half):
            arrived(qgv.at[0:48, 0:HALF], R_G2 + half)
            for s in (1, 2, 3):
                share_half(s, half, sibling, R_G3)

        slots(7, split_basis)
        until(T_G2[0])
        swap_half(0)
        until(T_H1)
        arrived(a1h.at[0:48], R_H1)
        assemble(a1h, qhv, F // 4)
        for s in (2, 1, 3):
            share_rows(qhv, 0, on2(s), S_H2, R_H2)
        share_rows(qhv, 0, sibling, S_H2, R_H3)
        split_basis(7)
        arrived(ebr.at[3:6], R_E2)
        ebs[2] = ebs[1] + ebr[3] + ebr[4] + ebr[5]
        post(ebs.at[2], ebr.at[6], sibling, S_E, R_E3)
        until(T_G3[0])
        project(0)
        until(T_G2[1])
        swap_half(1)
        until(T_G3[1])
        arrived(ebr.at[6:7], R_E3)
        ebs[3] = ebs[2] + ebr[6]
        project(1)
        damping = DAMP * jnp.sum(ebs[3][0:1], axis=1, keepdims=True) / K
        weighted = (accp[:, :128] + accp[:, 128:]) / (eigv[...] + damping)
        wmat[...] = weighted.T.astype(bf16)

        def expand(side, half):
            at = pl.ds(pl.multiple_of(side * 4096 + half * 2048, 2048), 2048)
            return jnp.dot(bhl[at, 0:128], wmat[...], preferred_element_type=f32)

        def block_rows(block, half):
            return pl.ds(pl.multiple_of(half * 2048 + block * KB, KB), KB)

        def give(half):
            at = pl.ds(half * 2048, 2048)
            part_out[at] = expand(1 - c, half).astype(bf16)
            post(part_out.at[at], part_in.at[at], sibling, S_BIG, R_PAIR + half)

        def keep(half):
            kept[pl.ds(half * 2048, 2048)] = expand(c, half)

        def add_pair(half):
            arrived(part_in.at[0:2048], R_PAIR + half)
            for s in (2, 1, 3, 0):
                at = block_rows(lax.rem(a1 + s, 4), half)
                total = kept[at] + part_in[at].astype(f32)
                if s:
                    r1s[at] = total.astype(bf16)
                    post(r1s.at[at], r1r.at[s - 1, pl.ds(half * KB, KB)], on1(s), S_BIG, R_R1 + half)
                else:
                    mine[pl.ds(half * KB, KB)] = total

        give(0)
        slots(1)
        give(1)
        keep(0)
        slots(1)
        keep(1)
        slots(1)
        add_pair(0)
        slots(1)
        add_pair(1)

        def match_hidden(j):
            for k in range(4):
                at = pl.ds(pl.multiple_of((4 * j + k) * 512, 512), 512)
                hm[...] += lax.dot_general(
                    hidv[:, at], qhv[:, at], (((1,), (1,)), ((), ())), preferred_element_type=f32
                )

        def sum_first(half):
            arrived(prec.at[0:3 * KB], R_R1 + half)
            for s in (2, 1, 3, 0):
                at = pl.ds(pl.multiple_of(half * KB + lax.rem(a2 + s, 4) * 128, 128), 128)
                total = mine[at] + r1r[0, at].astype(f32) + r1r[1, at].astype(f32) + r1r[2, at].astype(f32)
                if s:
                    r2s[at] = total.astype(bf16)
                    post(r2s.at[at], r2r.at[s - 1, pl.ds(half * 128, 128)], on2(s), S_SMALL, R_R2 + half)
                else:
                    mine[at] = total

        def sum_second(half):
            arrived(prec.at[0:384], R_R2 + half)
            at = pl.ds(pl.multiple_of(half * KB + a2 * 128, 128), 128)
            got = pl.ds(half * 128, 128)
            total = mine[at] + r2r[0, got].astype(f32) + r2r[1, got].astype(f32) + r2r[2, got].astype(f32)
            rows = pl.ds(pl.multiple_of(c * 4096 + half * 2048 + a1 * KB + a2 * 128, 128), 128)
            prec[rows] = total.astype(bf16)
            for s in (2, 1, 3):
                post(prec.at[rows], prec.at[rows], on2(s), S_SMALL, R_P1 + half)

        def band(s, half):
            return pl.ds(pl.multiple_of(c * 4096 + half * 2048 + lax.rem(a1 + 4 - s, 4) * KB, KB), KB)

        def gather_first(half):
            arrived(prec.at[0:384], R_P1 + half)
            rows = band(0, half)
            for s in (2, 1, 3):
                post(prec.at[rows], prec.at[rows], on1(s), S_BIG, R_P2 + 3 * half + s - 1)
            post(prec.at[rows], prec.at[rows], sibling, S_BIG, R_P3 + half)

        def gather_second(half):
            for s in (1, 3, 2):
                arrived(prec.at[0:KB], R_P2 + 3 * half + s - 1)
                rows = band(s, half)
                post(prec.at[rows], prec.at[rows], sibling, S_BIG, R_P3 + half)

        until(T_R1[0])
        sum_first(0)
        until(T_R1[1])
        sum_first(1)
        until(T_H2)
        arrived(qhv.at[0:48], R_H2)
        for s in (1, 2, 3):
            share_rows(qhv, s, sibling, S_H2, R_H3)
        for half in (0, 1):
            until(T_R2[half])
            sum_second(half)
        for half in (0, 1):
            until(T_P1[half])
            gather_first(half)
        until(T_H3)
        load_hid.wait()
        arrived(qhv.at[0:64], R_H3)
        pos = lax.broadcasted_iota(jnp.int32, (128, 128), 0)
        side = pos // 64
        p2nd = (pos // 16) % 4
        p1st = (pos // 4) % 4
        query = jnp.where(side == 0, p2nd * 2 + p1st // 2, p1st * 2 + p2nd // 2)
        pick[...] = (query == lax.broadcasted_iota(jnp.int32, (128, 128), 1)).astype(f32)
        hm[...] = jnp.zeros_like(hm)
        slots(F // 2048, match_hidden)

        gm[...] = jnp.zeros_like(gm)
        GROUP = KB // W

        def match_group(first):
            features = pl.ds(pl.multiple_of(first * W, KB), KB)
            gm[...] += jnp.dot(fin[:, features], prec[features], preferred_element_type=f32)

        def first_chunk(own_side, s, half):
            side, at = (c, a1) if own_side else (1 - c, a2)
            return side * (NCH // 2) + half * (NCH // 4) + lax.rem(at + 4 - s, 4) * GROUP

        def done_at(first):
            t = lax.rem(first + NZ * depth, NCH)
            other = NZ * (LAYERS - 1 - t // NZ) + lax.rem(t, NZ)
            return 2 * (jnp.where(t < NZ * depth, jnp.maximum(t, other), t) + GROUP - 1) + 1

        late = []

        def early(own_side, half):
            seen = now[0]
            if not CHAIN or seen >= SLOTS:
                for j in range(4):
                    match_group(first_chunk(own_side, j, half))
                return

            def two(j):
                for k in (0, 1):
                    first = first_chunk(own_side, 2 * j + k, half)

                    @pl.when(done_at(first) < seen)
                    def _(first=first):
                        match_group(first)

            slots(2, two)
            late.append((own_side, half, seen))

        until(T_P2[0])
        gather_second(0)
        early(True, 0)
        until(T_P2[1])
        gather_second(1)
        arrived(prec.at[0:2048], R_P3)
        early(False, 0)
        until(SLOTS)
        early(True, 1)
        for own_side, half, seen in late:
            for j in range(4):
                first = first_chunk(own_side, j, half)

                @pl.when(done_at(first) >= seen)
                def _(first=first):
                    match_group(first)

        arrived(prec.at[0:2048], R_P3 + 1)
        early(False, 1)
    else:
        load_bas.wait()
        load_hid.wait()
        until(SLOTS)

    if COL:
        prod = gm[...] * hm[...]
        sums = [jnp.sum(prod[s * SEQLEN:(s + 1) * SEQLEN], axis=0, keepdims=True) for s in (0, 1)]
        line = lax.broadcasted_iota(jnp.int32, (8, 128), 0)
        both = jnp.where(line == 0, sums[0], jnp.where(line == 1, sums[1], 0.0))
        tile = jnp.dot(both, pick[...], precision=lax.Precision.HIGHEST, preferred_element_type=f32)
        share[z] = tile / (SEQLEN * QLEN)
        for s in (4, 3, 5, 2, 6, 1, 7):
            remote(share.at[z], share.at[z], zs, zr, onz(s)).start()
        for like, kind in (
            (ebr, S_E),
            (a1g.at[0:48], S_G1),
            (a1h.at[0:48], S_H1),
            (qgv.at[0:112], S_G2),
            (qhv.at[0:112], S_H2),
            (bhl.at[0:7168], S_BIG),
            (prec.at[0:1536], S_SMALL),
        ):
            remote(like, like, cs.at[kind], cr.at[0], sibling).wait_send()
    if CHAIN:
        pltpu.make_async_copy(fin, out.at[0], out_sem).wait()

        @pl.when(z > 0)
        def _():
            sends = pl.ds(0, NCH - NZ)
            remote(down.at[sends], rcv.at[sends], chain_s, chain_r.at[0], onz(LAYERS - 1)).wait_send()

        @pl.when(z < LAYERS - 1)
        def _():
            sends = pl.ds(0, NUP - NZ)
            remote(ups.at[sends], upr.at[sends], up_s, up_r.at[0], onz(1)).wait_send()

        @pl.when(z == LAYERS - 1)
        def _():
            remote(ups, upr, up_s, up_r.at[0], onz(1)).wait_send()

    if COL:
        others = remote(share.at[0:LAYERS - 1], share.at[0:LAYERS - 1], zs, zr, sibling)
        others.wait_recv()
        total = share[0]
        for s in range(1, LAYERS):
            total = total + share[s]
        scores[...] = total[0:2, 0:8]
        others.wait_send()


def store(section, scores, section_out, scores_out, sem):
    rows = 128 // STORES
    copies = [
        pltpu.make_async_copy(section.at[0, pl.ds(k * rows, rows)], section_out.at[0, pl.ds(k * rows, rows)], sem.at[k])
        for k in range(STORES)
    ]
    copies.append(pltpu.make_async_copy(scores, scores_out, sem.at[STORES]))
    for copy in copies:
        copy.start()
    for copy in copies:
        copy.wait()


def column(incoming, hidden, basis, eigvals, query_grads, query_hidden):
    hbm = pl.BlockSpec(memory_space=pltpu.HBM)
    vmem = pl.BlockSpec(memory_space=pltpu.VMEM)
    dma = pltpu.SemaphoreType.DMA
    section, scores = pl.pallas_call(
        kernel,
        out_shape=(
            pltpu.VMEM((1, 128, D), bf16),
            pltpu.VMEM((2, 8), f32),
        ),
        in_specs=[hbm] * 6,
        out_specs=(pl.BlockSpec(memory_space=pl.ANY), vmem),
        scratch_shapes=[
            pltpu.VMEM((128, D), bf16),
            pltpu.VMEM((NCH, 128, W), bf16),
            pltpu.VMEM((NCH, 128, W), bf16),
            pltpu.VMEM((NUP, 128, W), bf16),
            pltpu.VMEM((NUP, 128, W), bf16),
            pltpu.VMEM((128, D), bf16),
            pltpu.VMEM((128, F), bf16),
            pltpu.VMEM((D, 128), f32),
            pltpu.VMEM((D, 256), bf16),
            pltpu.VMEM((1, 128), f32),
            pltpu.VMEM((1, 4, D), bf16),
            pltpu.VMEM((1, 4, F), bf16),
            pltpu.VMEM((16, D // 4), bf16),
            pltpu.VMEM((16, F // 4), bf16),
            pltpu.VMEM((64, D // 4), bf16),
            pltpu.VMEM((64, F // 4), bf16),
            pltpu.VMEM((128, D), bf16),
            pltpu.VMEM((128, F), bf16),
            pltpu.VMEM((4, 8, 128), f32),
            pltpu.VMEM((7, 8, 128), f32),
            pltpu.VMEM((4096, 128), bf16),
            pltpu.VMEM((4096, 128), bf16),
            pltpu.VMEM((4096, 128), f32),
            pltpu.VMEM((1024, 128), f32),
            pltpu.VMEM((4096, 128), bf16),
            pltpu.VMEM((3, 1024, 128), bf16),
            pltpu.VMEM((1024, 128), bf16),
            pltpu.VMEM((3, 256, 128), bf16),
            pltpu.VMEM((D, 128), bf16),
            pltpu.VMEM((128, 128), bf16),
            pltpu.VMEM((128, 256), f32),
            pltpu.VMEM((128, 128), f32),
            pltpu.VMEM((128, 128), f32),
            pltpu.VMEM((128, 128), f32),
            pltpu.VMEM((LAYERS, 8, 128), f32),
            dma((6,)),
            dma,
            dma,
            dma((AHEAD,)),
            dma,
            dma((NUP,)),
            dma((N_S,)),
            dma((N_R,)),
            dma,
            dma,
        ],
        compiler_params=pltpu.CompilerParams(
            collective_id=0, has_side_effects=True, vmem_limit_bytes=60 * 1024 * 1024
        ),
    )(incoming, hidden, basis, eigvals, query_grads, query_hidden)
    anyspace = pl.BlockSpec(memory_space=pl.ANY)
    return pl.pallas_call(
        store,
        out_shape=(
            jax.ShapeDtypeStruct((1, 128, D), bf16),
            jax.ShapeDtypeStruct((2, 8), f32),
        ),
        in_specs=[anyspace, anyspace],
        out_specs=(hbm, hbm),
        scratch_shapes=[dma((STORES + 1,))],
        compiler_params=pltpu.CompilerParams(vmem_limit_bytes=1024 * 1024),
    )(section, scores)


def solution(mesh):
    in_specs = (
        P("segment", "col", None),
        P("segment", "col", None),
        P("segment", None, "col"),
        P("segment", "col"),
        P("segment", "col", None),
        P("segment", "col", None),
    )
    out_specs = (P("segment", "col", None), P("col", None))
    return jax.shard_map(column, mesh=mesh, in_specs=in_specs, out_specs=out_specs, check_vma=False)
```
